256 devices in a mesh: lat: 16 (over x_hi, z), lon: 16 (over x_lo, y, core).
Axes of the slice: x: 4 (x_hi: 2, x_lo: 2; x = x_hi * 2 + x_lo), y: 4, z: 8, core: 2. Of those that a mesh axis runs over, the one named last changes fastest.
Arguments:
- fields: bfloat16 [4, 8, 96, 192, 192], P(None, None, 'lat', 'lon'), may hold values from -6 to 6
- norm1_gain: float32 [192], replicated, may hold values from 0.1 to 1.9
- w_qkv: bfloat16 [192, 576], replicated, may hold values from -0.4375 to 0.4375
- earth_bias: bfloat16 [4, 16, 6, 3312], P(None, 'lat'), may hold values from -5 to 5
- bias_index: int32 [144, 144], replicated, may hold values from 0 to 3311
- w_proj: bfloat16 [192, 192], replicated, may hold values from -0.4375 to 0.4375
- norm2_gain: float32 [192], replicated, may hold values from 0.1 to 1.9
- w_up: bfloat16 [192, 768], replicated, may hold values from -0.4375 to 0.4375
- w_down: bfloat16 [768, 192], replicated, may hold values from -0.21875 to 0.21875
- merge_gain: float32 [768], replicated, may hold values from 0.1 to 1.9
- w_merge: bfloat16 [768, 384], replicated, may hold values from -0.21875 to 0.21875
Outputs:
- merged: bfloat16 [4, 8, 48, 96, 384], P(None, None, 'lat', 'lon')
The draws below stay inside these ranges and needn't reach their ends.
All inputs are finite; a program needn't handle non-finite values.
Results may differ from the reference program's by a relative error of at most 0.015.
Values may be sent and summed in bfloat16 or wider, within the bound.
A program may use at most 128 MiB of HBM per device.

```python
import jax
import jax.numpy as jnp
from jax import lax

D = 192
HEADS = 6
FF = 768
LEVELS = 8
BIAS_ROWS = 3312
WINDOW = 144
BATCH = 4
LAT_TOTAL = 96
LON_TOTAL = 192
LAT_WINS = 16
MERGED = 384


def place_ends(drawn, own_key, smallest, largest):
    spot = [jax.random.randint(jax.random.fold_in(own_key, axis), (), 0, length) for axis, length in enumerate(drawn.shape)]
    main_axis = drawn.shape.index(max(drawn.shape))
    next_to = spot[:main_axis] + [(spot[main_axis] + 1) % drawn.shape[main_axis]] + spot[main_axis + 1:]
    return drawn.at[tuple(spot)].set(smallest).at[tuple(next_to)].set(largest)


def block_scale(stream_key, shape, cuts, smallest, high):
    factor_of, own = 1.0, jax.random.fold_in(stream_key, 6)
    for dim, blocks in cuts:
        draws = jnp.exp(jax.random.uniform(jax.random.fold_in(own, dim), (blocks,), jnp.float32, smallest / len(cuts), high / len(cuts)))
        factor_of = factor_of * jnp.repeat(draws, shape[dim] // blocks).reshape([-1 if axis == dim else 1 for axis in range(len(shape))])
    return factor_of


def normal_values(key, shape, scale, most, cuts=(), kind=jnp.bfloat16):
    values = jax.random.normal(key, shape, jnp.float32) * scale
    if len(cuts) > 0:
        values = block_scale(key, shape, cuts, -0.22, 0.18) * values
    return jnp.clip(values, min=-most, max=most).astype(kind)


def setup_inputs(seed: int = 0) -> dict:
    key_list = jax.random.split(jax.random.key(seed), 12)
    fields = normal_values(key_list[0], (BATCH, LEVELS, LAT_TOTAL, LON_TOTAL, D), 1.0, 6.0, ((2, 16), (3, 16)))
    norm1_gain = jnp.clip(1.0 + 0.18 * jax.random.normal(key_list[1], (D,), jnp.float32), 0.1, 1.9)
    w_qkv = normal_values(key_list[2], (D, 3 * D), D ** -0.5, 0.4375)
    earth_bias = normal_values(key_list[3], (LEVELS // 2, LAT_WINS, HEADS, BIAS_ROWS), 1.0, 5.0, ((1, 16),))
    bias_index = place_ends(jax.random.randint(key_list[4], (WINDOW, WINDOW), 0, BIAS_ROWS), jax.random.fold_in(key_list[4], 1), 0, BIAS_ROWS - 1).astype(jnp.int32)
    w_proj = normal_values(key_list[5], (D, D), D ** -0.5, 0.4375)
    norm2_gain = jnp.clip(1.0 + 0.18 * jax.random.normal(key_list[6], (D,), jnp.float32), 0.1, 1.9)
    w_up = normal_values(key_list[7], (D, FF), D ** -0.5, 0.4375)
    w_down = normal_values(key_list[8], (FF, D), FF ** -0.5, 0.21875)
    merge_gain = jnp.clip(1.0 + 0.18 * jax.random.normal(key_list[9], (4 * D,), jnp.float32), 0.1, 1.9)
    w_merge = normal_values(key_list[10], (4 * D, MERGED), (4 * D) ** -0.5, 0.21875)
    return {"fields": fields, "norm1_gain": norm1_gain, "w_qkv": w_qkv, "earth_bias": earth_bias, "bias_index": bias_index, "w_proj": w_proj, "norm2_gain": norm2_gain, "w_up": w_up, "w_down": w_down, "merge_gain": merge_gain, "w_merge": w_merge}


def layer_norm(inputs, gain_vec):
    values = inputs.astype(jnp.float32)
    average = lax.optimization_barrier(jnp.mean(values, -1, keepdims=True))
    centred = values - average
    spread = lax.optimization_barrier(jnp.mean(centred * centred, -1, keepdims=True))
    return centred * lax.rsqrt(spread + 1e-05) * gain_vec.astype(jnp.float32)

def window_labels(level_count, lat_wins, lat_anchor, lat_total):
    slot_index = jnp.arange(144)
    slot_level = slot_index // 72
    slot_lat = slot_index // 12 % 6
    level_index = 2 * jnp.arange(level_count // 2)[:, None] + slot_level[None, :]
    level_label = (level_index == level_count - 1).astype(jnp.int32)
    lat_rows = lat_anchor + 6 * jnp.arange(lat_wins)[:, None] + slot_lat[None, :]
    lat_label = (jnp.mod(lat_rows, lat_total) < 3).astype(jnp.int32)
    return 2 * level_label[:, None, :] + lat_label[None, :, :]

def attend(framed, norm1_gain, w_qkv, bias_slab, bias_index, w_proj, lat_anchor, lat_total):
    batch_size, level_count, row_count, col_count, feature_width = framed.shape
    head_count = bias_slab.shape[2]
    head_dim = feature_width // head_count
    lat_wins = row_count // 6
    lon_wins = col_count // 12
    level_wins = level_count // 2
    normed = layer_norm(framed, norm1_gain).astype(jnp.bfloat16)
    qkv_all = jnp.dot(normed.reshape(-1, feature_width), w_qkv, preferred_element_type=jnp.float32).astype(jnp.bfloat16)
    qkv_all = qkv_all.reshape(batch_size, level_wins, 2, lat_wins, 6, lon_wins, 12, 3 * feature_width)
    qkv_all = qkv_all.transpose(0, 1, 3, 5, 2, 4, 6, 7).reshape(batch_size * level_wins, lat_wins, lon_wins, 144, 3 * feature_width)
    bias_table = jnp.take(bias_slab, bias_index.reshape(-1), axis=3).reshape(level_wins, lat_wins, head_count, 144, 144)
    labels = window_labels(level_count, lat_wins, lat_anchor, lat_total)
    same_label = labels[:, :, :, None] == labels[:, :, None, :]
    group_level = jnp.tile(jnp.arange(level_wins), batch_size)
    score_scale = head_dim ** (-0.5)

    def one_group(group_item):
        window_block, level_group = group_item
        parts = window_block.astype(jnp.float32).reshape(lat_wins, lon_wins, 144, 3, head_count, head_dim)
        queries = parts[:, :, :, 0]
        keys_all = parts[:, :, :, 1]
        values_all = parts[:, :, :, 2]
        scores = jnp.einsum('lmqhe,lmkhe->lmhqk', queries, keys_all) * score_scale
        scores = scores + lax.dynamic_index_in_dim(bias_table, level_group, 0, False)[:, None].astype(jnp.float32)
        keep_mask = lax.dynamic_index_in_dim(same_label, level_group, 0, False)[:, None, None]
        weights = jnp.where(keep_mask, jnp.exp(scores), 0.0)
        probs = (weights / lax.optimization_barrier(jnp.sum(weights, -1, keepdims=True))).astype(jnp.bfloat16)
        result = jnp.einsum('lmhqk,lmkhe->lmqhe', probs.astype(jnp.float32), values_all).astype(jnp.bfloat16)
        return result.reshape(lat_wins, lon_wins, 144, feature_width)
    results = lax.map(one_group, (qkv_all, group_level))
    results = results.reshape(batch_size, level_wins, lat_wins, lon_wins, 2, 6, 12, feature_width)
    results = results.transpose(0, 1, 4, 2, 5, 3, 6, 7).reshape(framed.shape)
    projected = jnp.dot(results.reshape(-1, feature_width), w_proj, preferred_element_type=jnp.float32).reshape(framed.shape)
    return (framed.astype(jnp.float32) + projected).astype(jnp.bfloat16)

def mlp_merge(resid, norm2_gain, w_up, w_down, merge_gain, w_merge):
    batch_size, level_count, row_count, col_count, feature_width = resid.shape
    flat = resid.reshape(-1, feature_width)
    normed = layer_norm(flat, norm2_gain).astype(jnp.bfloat16)
    hidden = jax.nn.gelu(jnp.dot(normed, w_up, preferred_element_type=jnp.float32)).astype(jnp.bfloat16)
    block_out = (flat.astype(jnp.float32) + jnp.dot(hidden, w_down, preferred_element_type=jnp.float32)).astype(jnp.bfloat16)
    block_out = block_out.reshape(batch_size, level_count, row_count // 2, 2, col_count // 2, 2, feature_width)
    patches = block_out.transpose(0, 1, 2, 4, 5, 3, 6).reshape(-1, 4 * feature_width)
    pnorm = layer_norm(patches, merge_gain).astype(jnp.bfloat16)
    merged = jnp.dot(pnorm, w_merge, preferred_element_type=jnp.float32).astype(jnp.bfloat16)
    return merged.reshape(batch_size, level_count, row_count // 2, col_count // 2, w_merge.shape[1])

def reference(fields, norm1_gain, w_qkv, earth_bias, bias_index, w_proj, norm2_gain, w_up, w_down, merge_gain, w_merge):
    shifted = jnp.roll(fields, (-1, -3, -6), axis=(1, 2, 3))
    attended = attend(shifted, norm1_gain, w_qkv, earth_bias, bias_index, w_proj, jnp.int32(3), fields.shape[2])
    attended = jnp.roll(attended, (1, 3, 6), axis=(1, 2, 3))
    return mlp_merge(attended, norm2_gain, w_up, w_down, merge_gain, w_merge)
```

```python
import functools

import jax
import jax.numpy as jnp
from jax import lax
from jax.experimental import pallas as pl
from jax.experimental.pallas import tpu as pltpu
from jax.sharding import PartitionSpec as P

MESH = pl.DeviceIdType.MESH
F32 = jnp.float32
BF16 = jnp.bfloat16
I32 = jnp.int32
LOG2E = 1.4426950408889634
FIXED = 4096.0
HEADS = 6
WIN = 144
CHUNKS = 26
V_SCALE = 2.0**-8


def norm(values, gain):
    average = jnp.mean(values, -1, keepdims=True)
    centred = values - average
    spread = jnp.mean(centred * centred, -1, keepdims=True)
    return centred * lax.rsqrt(spread + 1e-05) * gain


def dot(a, b):
    return jnp.dot(a, b, preferred_element_type=F32)


def dot_nt(a, b):
    return lax.dot_general(a, b, (((1,), (1,)), ((), ())), preferred_element_type=F32)


def slot_label(slot, level_flag, lat_flag):
    level = jnp.where(slot >= 72, level_flag, 0)
    within = jnp.where(slot >= 72, slot - 72, slot)
    return 2 * level + jnp.where(within >= 36, lat_flag, 0)


def build_bias(is_last, table_v, index_v, rem_s, packed, single, biasx):
    packed[...] = jnp.zeros_like(packed)
    single[...] = jnp.zeros_like(single)
    for head in range(HEADS):
        fixed = jnp.round(table_v[head].astype(F32) * (LOG2E * FIXED)).astype(I32)
        for pair in range(2):
            low = fixed[2 * pair : 2 * pair + 1] & 0xFFFF
            high = fixed[2 * pair + 1 : 2 * pair + 2] << 16
            packed[pair * 8 + head : pair * 8 + head + 1, 0:3312] = low | high
            single[pair * HEADS + head, :, 0:3312] = low | high

    def finish(value, level_window, query, key):
        level_flag = jnp.where(level_window == 3, 1, 0)
        same = slot_label(query, level_flag, is_last) == slot_label(key, level_flag, is_last)
        return jnp.where(same, value.astype(F32) * (1.0 / FIXED), -1e30)

    def main_tile(step, carry):
        pair = step // HEADS
        head = step % HEADS
        for block in range(3):
            rows = slice(48 * block, 48 * block + 48)
            index = index_v[rows, 0:128]
            high, low = index >> 7, index & 127
            acc = jnp.zeros((48, 128), I32)
            for chunk in range(CHUNKS):
                source = single[step, :, 128 * chunk : 128 * chunk + 128]
                source = jnp.broadcast_to(source, (48, 128))
                got = jnp.take_along_axis(source, low, axis=1, mode="promise_in_bounds")
                acc = jnp.where(high == chunk, got, acc)
            query = lax.broadcasted_iota(I32, (48, 128), 0) + 48 * block
            key = lax.broadcasted_iota(I32, (48, 128), 1)
            biasx[2 * pair, head, rows, :] = finish((acc << 16) >> 16, 2 * pair, query, key)
            biasx[2 * pair + 1, head, rows, :] = finish(acc >> 16, 2 * pair + 1, query, key)
        return carry

    lax.fori_loop(0, 2 * HEADS, main_tile, 0)

    rem_s[...] = jnp.zeros_like(rem_s)
    rem_s[:, 0:16] = index_v[:, 128:144]
    sub = lax.broadcasted_iota(I32, (8, 128), 0)
    lane = lax.broadcasted_iota(I32, (8, 128), 1)
    turn = ((lane >> 4) - sub) & 7
    back = (lane + 16 * sub) & 127

    def rem_tile(group, carry):
        start = pl.multiple_of(group * 8, 8)
        placed = pltpu.roll(rem_s[pl.ds(start, 8), :].astype(F32), 0, 1, stride=16, stride_axis=0)
        index = jnp.broadcast_to(jnp.sum(placed, 0, keepdims=True), (8, 128)).astype(I32)
        high, low = index >> 7, index & 127
        for pair in range(2):
            acc = jnp.zeros((8, 128), I32)
            for chunk in range(CHUNKS):
                source = packed[8 * pair : 8 * pair + 8, 128 * chunk : 128 * chunk + 128]
                got = jnp.take_along_axis(source, low, axis=1, mode="promise_in_bounds")
                acc = jnp.where(high == chunk, got, acc)
            acc = pltpu.roll(acc, 0, 1, stride=16, stride_axis=0)
            acc = jnp.take_along_axis(acc, turn, axis=0, mode="promise_in_bounds")
            acc = jnp.take_along_axis(acc, back, axis=1, mode="promise_in_bounds")
            query = sub + start
            key = 128 + (lane & 15)
            biasx[2 * pair, HEADS, pl.ds(start, 8), :] = finish((acc << 16) >> 16, 2 * pair, query, key)
            biasx[2 * pair + 1, HEADS, pl.ds(start, 8), :] = finish(acc >> 16, 2 * pair + 1, query, key)
        return carry

    lax.fori_loop(0, WIN // 8, rem_tile, 0)


def kernel(
    n_lat,
    n_lon,
    x,
    g1,
    wqkv,
    table,
    index,
    wproj,
    g2,
    wup,
    wdown,
    gm,
    wmerge,
    out,
    frame,
    rs,
    mine,
    g1_v,
    wqkv_v,
    table_v,
    index_v,
    wproj_v,
    g2_v,
    wup_v,
    wdown_v,
    gm_v,
    wmerge_v,
    rem_s,
    packed,
    single,
    biasx,
    wq,
    wk,
    wv,
    wp,
    nrm,
    nw,
    q_s,
    k_s,
    v_s,
    at_s,
    out_v,
    fwd_send,
    fwd_recv,
    ret_send,
    ret_recv,
    own_sem,
    load_sem,
    out_sem,
):
    batch = x.shape[0]
    lat, lon = lax.axis_index("lat"), lax.axis_index("lon")
    up = lax.rem(lat + n_lat - 1, n_lat)
    down = lax.rem(lat + 1, n_lat)
    west = lax.rem(lon + n_lon - 1, n_lon)
    east = lax.rem(lon + 1, n_lon)
    before = ((up, lon), (lat, west), (up, west))
    after = ((down, lon), (lat, east), (down, east))

    barrier = pltpu.get_barrier_semaphore()
    for peer in before + after:
        pl.semaphore_signal(barrier, inc=1, device_id=peer, device_id_type=MESH)

    loads = [
        pltpu.make_async_copy(src, dst, load_sem.at[i])
        for i, (src, dst) in enumerate(
            (
                (index, index_v),
                (table, table_v),
                (g1, g1_v),
                (wqkv, wqkv_v),
                (wproj, wproj_v),
                (g2, g2_v),
                (wup, wup_v),
                (wdown, wdown_v),
                (gm, gm_v),
                (wmerge, wmerge_v),
            )
        )
    ]
    for load in loads:
        load.start()

    low3, high3 = pl.ds(0, 3), pl.ds(3, 3)
    low6, high6 = pl.ds(0, 6), pl.ds(6, 6)

    def own_copy(b):
        return pltpu.make_async_copy(x.at[b, high3, high6], frame.at[b, low3, low6], own_sem.at[b])

    fwd_pieces = (
        ((low3, high6), (high3, low6)),
        ((high3, low6), (low3, high6)),
        ((low3, low6), (high3, high6)),
    )

    def fwd_copy(b, i):
        (sr, sc), (dr, dc) = fwd_pieces[i]
        return pltpu.make_async_remote_copy(
            src_ref=x.at[b, sr, sc],
            dst_ref=frame.at[b, dr, dc],
            send_sem=fwd_send.at[b, i],
            recv_sem=fwd_recv.at[b, i],
            device_id=before[i],
            device_id_type=MESH,
        )

    def ret_copy(b, i):
        (dr, dc), (sr, sc) = fwd_pieces[i]
        return pltpu.make_async_remote_copy(
            src_ref=rs.at[b, sr, sc],
            dst_ref=mine.at[b, dr, dc],
            send_sem=ret_send.at[b, i],
            recv_sem=ret_recv.at[b, i],
            device_id=after[i],
            device_id_type=MESH,
        )

    for b in range(batch):
        own_copy(b).start()
    pl.semaphore_wait(barrier, 6)
    for b in range(batch):
        for i in range(3):
            fwd_copy(b, i).start()

    loads[0].wait()
    loads[1].wait()
    is_last = jnp.where(lat == n_lat - 1, 1, 0)
    build_bias(is_last, table_v, index_v, rem_s, packed, single, biasx)

    for load in loads[2:]:
        load.wait()
    wq[...] = wqkv_v[:, 0:192]
    wk[...] = wqkv_v[:, 192:384]
    wv[...] = jnp.zeros_like(wv)
    wv[:, 0:192] = wqkv_v[:, 384:576]
    wp[...] = jnp.zeros_like(wp)
    wp[:, 0:192] = wproj_v[...]

    lane192 = lax.broadcasted_iota(I32, (1, 192), 1)
    lane256 = lax.broadcasted_iota(I32, (1, 256), 1)
    key_masks = [jnp.where(lane192 // 32 == h, 1.0, 0.0).astype(BF16) for h in range(HEADS)]
    value_masks = [
        jnp.where((lane256 // 32 == h) & (lane256 < 192) | (lane256 == 192 + h), 1.0, 0.0).astype(BF16)
        for h in range(HEADS)
    ]
    ones_part = jnp.where(lane256 >= 192, V_SCALE, 0.0)
    den_lane = lax.broadcasted_iota(I32, (WIN, 128), 1) // 32

    def attend(b, carry):
        own_copy(b).wait()
        for i in range(3):
            fwd_copy(b, i).wait_recv()
        for r in range(6):
            tokens = frame[b, r].astype(F32).reshape(96, 192)
            tokens = norm(tokens, g1_v[...])
            nrm[0, r * 96 : r * 96 + 96, :] = tokens[:, 0:128]
            nrm[1, r * 96 : r * 96 + 96, 0:64] = tokens[:, 128:192]
        for w in range(4):
            first, second = 2 * w + 1, (2 * w + 2) % 8
            for half, width in ((0, 128), (1, 64)):
                part = [nrm[half, pl.ds(level, 72, stride=8), :] for level in (first, second)]
                part = jnp.concatenate(part, axis=0).astype(BF16)
                nw[w * WIN : w * WIN + WIN, 128 * half : 128 * half + width] = part[:, 0:width]
        tokens = nw[...]
        q_s[...] = (dot(tokens, wq[...]) * (LOG2E * 32.0**-0.5)).astype(BF16)
        k_s[...] = dot(tokens, wk[...]).astype(BF16)
        v_s[...] = (dot(tokens, wv[...]) * V_SCALE + ones_part).astype(BF16)
        for w in range(4):
            rows = slice(w * WIN, w * WIN + WIN)
            q, k, v = q_s[rows, :], k_s[rows, :], v_s[rows, :]
            probs = []
            values = []
            for tile in range(4):
                if tile < 3:
                    heads = (2 * tile, 2 * tile + 1)
                    keys = jnp.concatenate([k[0:128] * key_masks[h] for h in heads], axis=0)
                    values += [v[0:128] * value_masks[h] for h in heads]
                    bias = jnp.concatenate([biasx[w, h] for h in heads], axis=1)
                else:
                    keys = jnp.concatenate([k[128:144] * key_masks[h] for h in range(HEADS)], axis=0)
                    values += [v[128:144] * value_masks[h] for h in range(HEADS)]
                    bias = biasx[w, HEADS][:, 0:96]
                probs.append(jnp.exp2(dot_nt(q, keys) + bias).astype(BF16))
            summed = dot(jnp.concatenate(probs, axis=1), jnp.concatenate(values, axis=0))
            left, right = summed[:, 0:128], summed[:, 128:256]
            inverse = 1.0 / right
            left_den = jnp.take_along_axis(inverse, 64 + den_lane, axis=1, mode="promise_in_bounds")
            right_den = jnp.take_along_axis(inverse, 64 + 4 + (den_lane & 1), axis=1, mode="promise_in_bounds")
            at_s[rows, 0:128] = (left * left_den).astype(BF16)
            at_s[rows, 128:192] = (right * right_den)[:, 0:64].astype(BF16)
        projected = dot(at_s[...], wp[...])
        for w in range(4):
            first, second = 2 * w + 1, (2 * w + 2) % 8
            for half in range(2):
                lanes = slice(128 * half, 128 * half + 128)
                nrm[half, pl.ds(first, 72, stride=8), :] = projected[w * WIN : w * WIN + 72, lanes]
                nrm[half, pl.ds(second, 72, stride=8), :] = projected[w * WIN + 72 : w * WIN + 144, lanes]
        for r in range(6):
            rows = slice(r * 96, r * 96 + 96)
            added = jnp.concatenate([nrm[0, rows, :], nrm[1, rows, 0:64]], axis=1)
            total = (frame[b, r].astype(F32) + added.reshape(12, 8, 192)).astype(BF16)
            rs[b, r] = total
            if r < 3:
                mine[b, 3 + r, 6:12] = total[0:6]
        for i in range(3):
            ret_copy(b, i).start()
        return carry

    lax.fori_loop(0, batch, attend, 0)

    def out_copy(b):
        return pltpu.make_async_copy(out_v.at[b], out.at[b], out_sem.at[b])

    def feed(b, carry):
        for i in range(3):
            ret_copy(b, i).wait_recv()
        flat = mine[b].astype(F32).reshape(576, 192)
        normed = norm(flat, g2_v[...]).astype(BF16)
        block = flat
        for j in range(3):
            hidden = jax.nn.gelu(dot(normed, wup_v[:, 256 * j : 256 * j + 256])).astype(BF16)
            block = block + dot_nt(hidden, wdown_v[:, 256 * j : 256 * j + 256])
        block = block.astype(BF16).astype(F32).reshape(3, 2, 6, 2, 8, 192)
        parts = [block[:, i, :, j].reshape(144, 192) for j in range(2) for i in range(2)]
        average = sum(jnp.sum(p, -1, keepdims=True) for p in parts) * (1.0 / 768)
        parts = [p - average for p in parts]
        spread = sum(jnp.sum(p * p, -1, keepdims=True) for p in parts) * (1.0 / 768)
        scale = lax.rsqrt(spread + 1e-05)
        merged = jnp.zeros((144, 384), F32)
        for i, p in enumerate(parts):
            normed = (p * scale * gm_v[:, 192 * i : 192 * i + 192]).astype(BF16)
            merged = merged + dot(normed, wmerge_v[192 * i : 192 * i + 192, :])
        out_v[b] = merged.reshape(3, 6, 8, 384).astype(BF16)
        out_copy(b).start()
        return carry

    lax.fori_loop(0, batch, feed, 0)

    for b in range(batch):
        out_copy(b).wait()
        for i in range(3):
            fwd_copy(b, i).wait_send()
            ret_copy(b, i).wait_send()


def body(fields, norm1_gain, w_qkv, earth_bias, bias_index, w_proj, norm2_gain, w_up, w_down, merge_gain, w_merge):
    batch = fields.shape[0]
    args = (
        fields.transpose(0, 2, 3, 1, 4),
        norm1_gain.reshape(1, 192),
        w_qkv,
        earth_bias.transpose(1, 2, 0, 3).reshape(6, 4, 3312),
        bias_index,
        w_proj,
        norm2_gain.reshape(1, 192),
        w_up,
        w_down.T,
        merge_gain.reshape(1, 768),
        w_merge,
    )
    block = (batch, 6, 12, 8, 192)
    shapes = [a.shape for a in args]
    dtypes = [a.dtype for a in args]
    loaded = [pltpu.VMEM(s, d) for s, d in zip(shapes[1:], dtypes[1:])]
    merged = pl.pallas_call(
        functools.partial(kernel, lax.axis_size("lat"), lax.axis_size("lon")),
        out_shape=jax.ShapeDtypeStruct((batch, 3, 6, 8, 384), BF16),
        in_specs=[pl.BlockSpec(memory_space=pl.ANY)] * len(args),
        out_specs=pl.BlockSpec(memory_space=pl.ANY),
        scratch_shapes=[
            pltpu.VMEM(block, BF16),
            pltpu.VMEM(block, BF16),
            pltpu.VMEM(block, BF16),
            *loaded,
            pltpu.VMEM((WIN, 128), I32),
            pltpu.VMEM((16, 128 * CHUNKS), I32),
            pltpu.VMEM((2 * HEADS, 1, 128 * CHUNKS), I32),
            pltpu.VMEM((4, 7, WIN, 128), F32),
            pltpu.VMEM((192, 192), BF16),
            pltpu.VMEM((192, 192), BF16),
            pltpu.VMEM((192, 256), BF16),
            pltpu.VMEM((192, 256), BF16),
            pltpu.VMEM((2, 576, 128), F32),
            pltpu.VMEM((576, 192), BF16),
            pltpu.VMEM((576, 192), BF16),
            pltpu.VMEM((576, 192), BF16),
            pltpu.VMEM((576, 256), BF16),
            pltpu.VMEM((576, 192), BF16),
            pltpu.VMEM((batch, 3, 6, 8, 384), BF16),
            pltpu.SemaphoreType.DMA((batch, 3)),
            pltpu.SemaphoreType.DMA((batch, 3)),
            pltpu.SemaphoreType.DMA((batch, 3)),
            pltpu.SemaphoreType.DMA((batch, 3)),
            pltpu.SemaphoreType.DMA((batch,)),
            pltpu.SemaphoreType.DMA((10,)),
            pltpu.SemaphoreType.DMA((batch,)),
        ],
        compiler_params=pltpu.CompilerParams(
            collective_id=0, has_side_effects=True, vmem_limit_bytes=56 * 1024 * 1024
        ),
    )(*args)
    return merged.transpose(0, 3, 1, 2, 4)


def solution(mesh):
    in_specs = (
        P(None, None, "lat", "lon", None),
        P(),
        P(),
        P(None, "lat", None, None),
        P(),
        P(),
        P(),
        P(),
        P(),
        P(),
        P(),
    )
    out_specs = P(None, None, "lat", "lon", None)
    return jax.shard_map(body, mesh=mesh, in_specs=in_specs, out_specs=out_specs, check_vma=False)
```

```python
import functools

import jax
import jax.numpy as jnp
from jax import lax
from jax.experimental import pallas as pl
from jax.experimental.pallas import tpu as pltpu
from jax.sharding import PartitionSpec as P

MESH = pl.DeviceIdType.MESH
F32 = jnp.float32
BF16 = jnp.bfloat16
I32 = jnp.int32
LOG2E = 1.4426950408889634
FIXED = 4096.0
HEADS = 6
WIN = 144
CHUNKS = 26
V_SCALE = 2.0**-8


def norm(values, gain):
    average = jnp.mean(values, -1, keepdims=True)
    centred = values - average
    spread = jnp.mean(centred * centred, -1, keepdims=True)
    return centred * lax.rsqrt(spread + 1e-05) * gain


def dot(a, b):
    return jnp.dot(a, b, preferred_element_type=F32)


def dot_nt(a, b):
    return lax.dot_general(a, b, (((1,), (1,)), ((), ())), preferred_element_type=F32)


def slot_label(slot, level_flag, lat_flag):
    level = jnp.where(slot >= 72, level_flag, 0)
    within = jnp.where(slot >= 72, slot - 72, slot)
    return 2 * level + jnp.where(within >= 36, lat_flag, 0)


def prepare_tables(table_v, packed, single):
    packed[...] = jnp.zeros_like(packed)
    single[...] = jnp.zeros_like(single)
    for head in range(HEADS):
        fixed = jnp.round(table_v[head].astype(F32) * (LOG2E * FIXED)).astype(I32)
        for pair in range(2):
            low = fixed[2 * pair : 2 * pair + 1] & 0xFFFF
            high = fixed[2 * pair + 1 : 2 * pair + 2] << 16
            packed[pair, head : head + 1, 0:3312] = low | high
            single[pair, head, :, 0:3312] = low | high


def gather_groups(first, count, pair, index_v, rem_s, packed, single, raw):
    sub = lax.broadcasted_iota(I32, (8, 128), 0)
    lane = lax.broadcasted_iota(I32, (8, 128), 1)
    turn = ((lane >> 4) - sub) & 7
    back = (lane + 16 * sub) & 127

    def one_group(group, carry):
        start = pl.multiple_of(group * 8, 8)
        index = index_v[pl.ds(start, 8), 0:128]
        high, low = index >> 7, index & 127
        placed = pltpu.roll(rem_s[pl.ds(start, 8), :].astype(F32), 0, 1, stride=16, stride_axis=0)
        rem = jnp.broadcast_to(jnp.sum(placed, 0, keepdims=True), (8, 128)).astype(I32)
        rem_high, rem_low = rem >> 7, rem & 127
        accs = [jnp.zeros((8, 128), I32) for _ in range(HEADS + 1)]
        for chunk in range(CHUNKS):
            lanes = slice(128 * chunk, 128 * chunk + 128)
            here = high == chunk
            for head in range(HEADS):
                source = jnp.broadcast_to(single[pair, head, :, lanes], (8, 128))
                got = jnp.take_along_axis(source, low, axis=1, mode="promise_in_bounds")
                accs[head] = jnp.where(here, got, accs[head])
            got = jnp.take_along_axis(packed[pair, :, lanes], rem_low, axis=1, mode="promise_in_bounds")
            accs[HEADS] = jnp.where(rem_high == chunk, got, accs[HEADS])
        acc = pltpu.roll(accs[HEADS], 0, 1, stride=16, stride_axis=0)
        acc = jnp.take_along_axis(acc, turn, axis=0, mode="promise_in_bounds")
        accs[HEADS] = jnp.take_along_axis(acc, back, axis=1, mode="promise_in_bounds")
        for tile in range(HEADS + 1):
            raw[pair, tile, pl.ds(start, 8), :] = accs[tile]
        return carry

    lax.fori_loop(first, first + count, one_group, 0)


def finish_bias(pair, is_last, raw, biasx):
    for rows in range(0, WIN, 48):
        query = lax.broadcasted_iota(I32, (48, 128), 0) + rows
        lane = lax.broadcasted_iota(I32, (48, 128), 1)
        for key, tiles in ((lane, range(HEADS)), (128 + (lane & 15), (HEADS,))):
            for half in range(2):
                level_flag = jnp.where(pair == 1, half, 0)
                same = slot_label(query, level_flag, is_last) == slot_label(key, level_flag, is_last)
                for tile in tiles:
                    value = raw[pair, tile, rows : rows + 48, :]
                    value = (value >> 16) if half else ((value << 16) >> 16)
                    value = value.astype(F32) * (1.0 / FIXED)
                    biasx[2 * pair + half, tile, rows : rows + 48, :] = jnp.where(same, value, -1e30)


def kernel(
    n_lat,
    n_lon,
    x,
    g1,
    wqkv,
    table,
    index,
    wproj,
    g2,
    wup,
    wdown,
    gm,
    wmerge,
    out,
    frame,
    rs,
    mine,
    g1_v,
    wqkv_v,
    table_v,
    index_v,
    wproj_v,
    g2_v,
    wup_v,
    wdown_v,
    gm_v,
    wmerge_v,
    rem_s,
    packed,
    single,
    raw,
    biasx,
    wq,
    wk,
    wv,
    wp,
    nrm,
    nw,
    q_s,
    k_s,
    v_s,
    at_s,
    out_v,
    fwd_send,
    fwd_recv,
    ret_send,
    ret_recv,
    table_send,
    table_recv,
    own_sem,
    load_sem,
    out_sem,
):
    batch = x.shape[0]
    lat, lon = lax.axis_index("lat"), lax.axis_index("lon")
    up = lax.rem(lat + n_lat - 1, n_lat)
    down = lax.rem(lat + 1, n_lat)
    west = lax.rem(lon + n_lon - 1, n_lon)
    east = lax.rem(lon + 1, n_lon)
    before = ((up, lon), (lat, west), (up, west))
    after = ((down, lon), (lat, east), (down, east))

    barrier = pltpu.get_barrier_semaphore()
    for peer in before + after:
        pl.semaphore_signal(barrier, inc=1, device_id=peer, device_id_type=MESH)

    loads = [
        pltpu.make_async_copy(src, dst, load_sem.at[i])
        for i, (src, dst) in enumerate(
            (
                (index, index_v),
                (table, table_v),
                (g1, g1_v),
                (wqkv, wqkv_v),
                (wproj, wproj_v),
                (g2, g2_v),
                (wup, wup_v),
                (wdown, wdown_v),
                (gm, gm_v),
                (wmerge, wmerge_v),
            )
        )
    ]
    for load in loads:
        load.start()

    low3, high3 = pl.ds(0, 3), pl.ds(3, 3)
    low6, high6 = pl.ds(0, 6), pl.ds(6, 6)

    def own_copy(b):
        return pltpu.make_async_copy(x.at[b, high3, high6], frame.at[b, low3, low6], own_sem.at[b])

    fwd_pieces = (
        ((low3, high6), (high3, low6)),
        ((high3, low6), (low3, high6)),
        ((low3, low6), (high3, high6)),
    )

    def fwd_copy(b, i):
        (sr, sc), (dr, dc) = fwd_pieces[i]
        return pltpu.make_async_remote_copy(
            src_ref=x.at[b, sr, sc],
            dst_ref=frame.at[b, dr, dc],
            send_sem=fwd_send.at[b, i],
            recv_sem=fwd_recv.at[b, i],
            device_id=before[i],
            device_id_type=MESH,
        )

    def ret_copy(b, i):
        (dr, dc), (sr, sc) = fwd_pieces[i]
        return pltpu.make_async_remote_copy(
            src_ref=rs.at[b, sr, sc],
            dst_ref=mine.at[b, dr, dc],
            send_sem=ret_send.at[b, i],
            recv_sem=ret_recv.at[b, i],
            device_id=after[i],
            device_id_type=MESH,
        )

    for b in range(batch):
        own_copy(b).start()
    pl.semaphore_wait(barrier, 6)
    for b in range(batch):
        for i in range(3):
            fwd_copy(b, i).start()

    loads[0].wait()
    loads[1].wait()
    is_last = jnp.where(lat == n_lat - 1, 1, 0)
    prepare_tables(table_v, packed, single)
    rem_s[...] = jnp.zeros_like(rem_s)
    rem_s[:, 0:16] = index_v[:, 128:144]
    pair = lon % 2
    twin = (lat, lon + 1 - 2 * pair)

    def table_copy(part, which):
        piece = raw.at[which, :, pl.ds(48 * part, 48)]
        return pltpu.make_async_remote_copy(
            src_ref=piece,
            dst_ref=piece,
            send_sem=table_send.at[part],
            recv_sem=table_recv.at[part],
            device_id=twin,
            device_id_type=MESH,
        )

    for part in range(3):
        gather_groups(6 * part, 6, pair, index_v, rem_s, packed, single, raw)
        table_copy(part, pair).start()
    finish_bias(pair, is_last, raw, biasx)
    for part in range(3):
        table_copy(part, 1 - pair).wait_recv()
    finish_bias(1 - pair, is_last, raw, biasx)

    for load in loads[2:]:
        load.wait()
    wq[...] = wqkv_v[:, 0:192]
    wk[...] = wqkv_v[:, 192:384]
    wv[...] = jnp.zeros_like(wv)
    wv[:, 0:192] = wqkv_v[:, 384:576]
    wp[...] = jnp.zeros_like(wp)
    wp[:, 0:192] = wproj_v[...]

    lane192 = lax.broadcasted_iota(I32, (1, 192), 1)
    lane256 = lax.broadcasted_iota(I32, (1, 256), 1)
    key_masks = [jnp.where(lane192 // 32 == h, 1.0, 0.0).astype(BF16) for h in range(HEADS)]
    value_masks = [
        jnp.where((lane256 // 32 == h) & (lane256 < 192) | (lane256 == 192 + h), 1.0, 0.0).astype(BF16)
        for h in range(HEADS)
    ]
    ones_part = jnp.where(lane256 >= 192, V_SCALE, 0.0)
    den_lane = lax.broadcasted_iota(I32, (WIN, 128), 1) // 32

    def attend(b, carry):
        own_copy(b).wait()
        for i in range(3):
            fwd_copy(b, i).wait_recv()
        for r in range(6):
            tokens = frame[b, r].astype(F32).reshape(96, 192)
            tokens = norm(tokens, g1_v[...])
            nrm[0, r * 96 : r * 96 + 96, :] = tokens[:, 0:128]
            nrm[1, r * 96 : r * 96 + 96, 0:64] = tokens[:, 128:192]
        for w in range(4):
            first, second = 2 * w + 1, (2 * w + 2) % 8
            for half, width in ((0, 128), (1, 64)):
                part = [nrm[half, pl.ds(level, 72, stride=8), :] for level in (first, second)]
                part = jnp.concatenate(part, axis=0).astype(BF16)
                nw[w * WIN : w * WIN + WIN, 128 * half : 128 * half + width] = part[:, 0:width]
        tokens = nw[...]
        q_s[...] = (dot(tokens, wq[...]) * (LOG2E * 32.0**-0.5)).astype(BF16)
        k_s[...] = dot(tokens, wk[...]).astype(BF16)
        v_s[...] = (dot(tokens, wv[...]) * V_SCALE + ones_part).astype(BF16)
        for w in range(4):
            rows = slice(w * WIN, w * WIN + WIN)
            q, k, v = q_s[rows, :], k_s[rows, :], v_s[rows, :]
            probs = []
            values = []
            for tile in range(4):
                if tile < 3:
                    heads = (2 * tile, 2 * tile + 1)
                    keys = jnp.concatenate([k[0:128] * key_masks[h] for h in heads], axis=0)
                    values += [v[0:128] * value_masks[h] for h in heads]
                    bias = jnp.concatenate([biasx[w, h] for h in heads], axis=1)
                else:
                    keys = jnp.concatenate([k[128:144] * key_masks[h] for h in range(HEADS)], axis=0)
                    values += [v[128:144] * value_masks[h] for h in range(HEADS)]
                    bias = biasx[w, HEADS][:, 0:96]
                probs.append(jnp.exp2(dot_nt(q, keys) + bias).astype(BF16))
            summed = dot(jnp.concatenate(probs, axis=1), jnp.concatenate(values, axis=0))
            left, right = summed[:, 0:128], summed[:, 128:256]
            inverse = 1.0 / right
            left_den = jnp.take_along_axis(inverse, 64 + den_lane, axis=1, mode="promise_in_bounds")
            right_den = jnp.take_along_axis(inverse, 64 + 4 + (den_lane & 1), axis=1, mode="promise_in_bounds")
            at_s[rows, 0:128] = (left * left_den).astype(BF16)
            at_s[rows, 128:192] = (right * right_den)[:, 0:64].astype(BF16)
        projected = dot(at_s[...], wp[...])
        for w in range(4):
            first, second = 2 * w + 1, (2 * w + 2) % 8
            for half in range(2):
                lanes = slice(128 * half, 128 * half + 128)
                nrm[half, pl.ds(first, 72, stride=8), :] = projected[w * WIN : w * WIN + 72, lanes]
                nrm[half, pl.ds(second, 72, stride=8), :] = projected[w * WIN + 72 : w * WIN + 144, lanes]
        for r in range(6):
            rows = slice(r * 96, r * 96 + 96)
            added = jnp.concatenate([nrm[0, rows, :], nrm[1, rows, 0:64]], axis=1)
            total = (frame[b, r].astype(F32) + added.reshape(12, 8, 192)).astype(BF16)
            rs[b, r] = total
            if r < 3:
                mine[b, 3 + r, 6:12] = total[0:6]
        for i in range(3):
            ret_copy(b, i).start()
        return carry

    lax.fori_loop(0, batch, attend, 0)

    def out_copy(b):
        return pltpu.make_async_copy(out_v.at[b], out.at[b], out_sem.at[b])

    def feed(b, carry):
        for i in range(3):
            ret_copy(b, i).wait_recv()
        flat = mine[b].astype(F32).reshape(576, 192)
        normed = norm(flat, g2_v[...]).astype(BF16)
        block = flat
        for j in range(3):
            hidden = jax.nn.gelu(dot(normed, wup_v[:, 256 * j : 256 * j + 256])).astype(BF16)
            block = block + dot_nt(hidden, wdown_v[:, 256 * j : 256 * j + 256])
        block = block.astype(BF16).astype(F32).reshape(3, 2, 6, 2, 8, 192)
        parts = [block[:, i, :, j].reshape(144, 192) for j in range(2) for i in range(2)]
        average = sum(jnp.sum(p, -1, keepdims=True) for p in parts) * (1.0 / 768)
        parts = [p - average for p in parts]
        spread = sum(jnp.sum(p * p, -1, keepdims=True) for p in parts) * (1.0 / 768)
        scale = lax.rsqrt(spread + 1e-05)
        merged = jnp.zeros((144, 384), F32)
        for i, p in enumerate(parts):
            normed = (p * scale * gm_v[:, 192 * i : 192 * i + 192]).astype(BF16)
            merged = merged + dot(normed, wmerge_v[192 * i : 192 * i + 192, :])
        out_v[b] = merged.reshape(3, 6, 8, 384).astype(BF16)
        out_copy(b).start()
        return carry

    lax.fori_loop(0, batch, feed, 0)

    for part in range(3):
        table_copy(part, pair).wait_send()
    for b in range(batch):
        out_copy(b).wait()
        for i in range(3):
            fwd_copy(b, i).wait_send()
            ret_copy(b, i).wait_send()


def body(fields, norm1_gain, w_qkv, earth_bias, bias_index, w_proj, norm2_gain, w_up, w_down, merge_gain, w_merge):
    batch = fields.shape[0]
    args = (
        fields.transpose(0, 2, 3, 1, 4),
        norm1_gain.reshape(1, 192),
        w_qkv,
        earth_bias.transpose(1, 2, 0, 3).reshape(6, 4, 3312),
        bias_index,
        w_proj,
        norm2_gain.reshape(1, 192),
        w_up,
        w_down.T,
        merge_gain.reshape(1, 768),
        w_merge,
    )
    block = (batch, 6, 12, 8, 192)
    shapes = [a.shape for a in args]
    dtypes = [a.dtype for a in args]
    loaded = [pltpu.VMEM(s, d) for s, d in zip(shapes[1:], dtypes[1:])]
    merged = pl.pallas_call(
        functools.partial(kernel, lax.axis_size("lat"), lax.axis_size("lon")),
        out_shape=jax.ShapeDtypeStruct((batch, 3, 6, 8, 384), BF16),
        in_specs=[pl.BlockSpec(memory_space=pl.ANY)] * len(args),
        out_specs=pl.BlockSpec(memory_space=pl.ANY),
        scratch_shapes=[
            pltpu.VMEM(block, BF16),
            pltpu.VMEM(block, BF16),
            pltpu.VMEM(block, BF16),
            *loaded,
            pltpu.VMEM((WIN, 128), I32),
            pltpu.VMEM((2, 8, 128 * CHUNKS), I32),
            pltpu.VMEM((2, HEADS, 1, 128 * CHUNKS), I32),
            pltpu.VMEM((2, 7, WIN, 128), I32),
            pltpu.VMEM((4, 7, WIN, 128), F32),
            pltpu.VMEM((192, 192), BF16),
            pltpu.VMEM((192, 192), BF16),
            pltpu.VMEM((192, 256), BF16),
            pltpu.VMEM((192, 256), BF16),
            pltpu.VMEM((2, 576, 128), F32),
            pltpu.VMEM((576, 192), BF16),
            pltpu.VMEM((576, 192), BF16),
            pltpu.VMEM((576, 192), BF16),
            pltpu.VMEM((576, 256), BF16),
            pltpu.VMEM((576, 192), BF16),
            pltpu.VMEM((batch, 3, 6, 8, 384), BF16),
            pltpu.SemaphoreType.DMA((batch, 3)),
            pltpu.SemaphoreType.DMA((batch, 3)),
            pltpu.SemaphoreType.DMA((batch, 3)),
            pltpu.SemaphoreType.DMA((batch, 3)),
            pltpu.SemaphoreType.DMA((3,)),
            pltpu.SemaphoreType.DMA((3,)),
            pltpu.SemaphoreType.DMA((batch,)),
            pltpu.SemaphoreType.DMA((10,)),
            pltpu.SemaphoreType.DMA((batch,)),
        ],
        compiler_params=pltpu.CompilerParams(
            collective_id=0, has_side_effects=True, vmem_limit_bytes=56 * 1024 * 1024
        ),
    )(*args)
    return merged.transpose(0, 3, 1, 2, 4)


def solution(mesh):
    in_specs = (
        P(None, None, "lat", "lon", None),
        P(),
        P(),
        P(None, "lat", None, None),
        P(),
        P(),
        P(),
        P(),
        P(),
        P(),
        P(),
    )
    out_specs = P(None, None, "lat", "lon", None)
    return jax.shard_map(body, mesh=mesh, in_specs=in_specs, out_specs=out_specs, check_vma=False)
```

```python
import functools

import jax
import jax.numpy as jnp
from jax import lax
from jax.experimental import pallas as pl
from jax.experimental.pallas import tpu as pltpu
from jax.sharding import PartitionSpec as P

MESH = pl.DeviceIdType.MESH
F32 = jnp.float32
BF16 = jnp.bfloat16
I32 = jnp.int32
LOG2E = 1.4426950408889634
FIXED = 4096.0
HEADS = 6
WIN = 144
CHUNKS = 26
V_SCALE = 2.0**-8


def norm(values, gain):
    average = jnp.mean(values, -1, keepdims=True)
    centred = values - average
    spread = jnp.mean(centred * centred, -1, keepdims=True)
    return centred * lax.rsqrt(spread + 1e-05) * gain


def dot(a, b):
    return jnp.dot(a, b, preferred_element_type=F32)


def dot_nt(a, b):
    return lax.dot_general(a, b, (((1,), (1,)), ((), ())), preferred_element_type=F32)


def pack(piece, target):
    target[0:18] = piece[:, :, 0:128]
    target[18:27] = jnp.concatenate([piece[0:9, :, 128:192], piece[9:18, :, 128:192]], axis=2)


def unpack(tiles):
    tiles = tiles.astype(F32)
    last = jnp.concatenate([tiles[18:27, :, 0:64], tiles[18:27, :, 64:128]], axis=0)
    return jnp.concatenate([tiles[0:18], last], axis=2).reshape(144, 192)


def slot_label(slot, level_flag, lat_flag):
    level = jnp.where(slot >= 72, level_flag, 0)
    within = jnp.where(slot >= 72, slot - 72, slot)
    return 2 * level + jnp.where(within >= 36, lat_flag, 0)


def prepare_tables(table_v, packed, single):
    packed[...] = jnp.zeros_like(packed)
    single[...] = jnp.zeros_like(single)
    for head in range(HEADS):
        fixed = jnp.round(table_v[head].astype(F32) * (LOG2E * FIXED)).astype(I32)
        for pair in range(2):
            low = fixed[2 * pair : 2 * pair + 1] & 0xFFFF
            high = fixed[2 * pair + 1 : 2 * pair + 2] << 16
            packed[pair, head : head + 1, 0:3312] = low | high
            single[pair, head, :, 0:3312] = low | high


def gather_groups(first, count, pair, index_v, rem_s, packed, single, raw):
    sub = lax.broadcasted_iota(I32, (8, 128), 0)
    lane = lax.broadcasted_iota(I32, (8, 128), 1)
    turn = ((lane >> 4) - sub) & 7
    back = (lane + 16 * sub) & 127

    def one_group(group, carry):
        start = pl.multiple_of(group * 8, 8)
        index = index_v[pl.ds(start, 8), 0:128]
        high, low = index >> 7, index & 127
        placed = pltpu.roll(rem_s[pl.ds(start, 8), :].astype(F32), 0, 1, stride=16, stride_axis=0)
        rem = jnp.broadcast_to(jnp.sum(placed, 0, keepdims=True), (8, 128)).astype(I32)
        rem_high, rem_low = rem >> 7, rem & 127
        accs = [jnp.zeros((8, 128), I32) for _ in range(HEADS + 1)]
        for chunk in range(CHUNKS):
            lanes = slice(128 * chunk, 128 * chunk + 128)
            here = high == chunk
            for head in range(HEADS):
                source = jnp.broadcast_to(single[pair, head, :, lanes], (8, 128))
                got = jnp.take_along_axis(source, low, axis=1, mode="promise_in_bounds")
                accs[head] = jnp.where(here, got, accs[head])
            got = jnp.take_along_axis(packed[pair, :, lanes], rem_low, axis=1, mode="promise_in_bounds")
            accs[HEADS] = jnp.where(rem_high == chunk, got, accs[HEADS])
        acc = pltpu.roll(accs[HEADS], 0, 1, stride=16, stride_axis=0)
        acc = jnp.take_along_axis(acc, turn, axis=0, mode="promise_in_bounds")
        accs[HEADS] = jnp.take_along_axis(acc, back, axis=1, mode="promise_in_bounds")
        for tile in range(HEADS + 1):
            raw[pair, tile, pl.ds(start, 8), :] = accs[tile]
        return carry

    lax.fori_loop(first, first + count, one_group, 0)


def finish_bias(pair, is_last, raw, biasx):
    for rows in range(0, WIN, 48):
        query = lax.broadcasted_iota(I32, (48, 128), 0) + rows
        lane = lax.broadcasted_iota(I32, (48, 128), 1)
        for key, tiles in ((lane, range(HEADS)), (128 + (lane & 15), (HEADS,))):
            for half in range(2):
                level_flag = jnp.where(pair == 1, half, 0)
                same = slot_label(query, level_flag, is_last) == slot_label(key, level_flag, is_last)
                for tile in tiles:
                    value = raw[pair, tile, rows : rows + 48, :]
                    value = (value >> 16) if half else ((value << 16) >> 16)
                    value = value.astype(F32) * (1.0 / FIXED)
                    biasx[2 * pair + half, tile, rows : rows + 48, :] = jnp.where(same, value, -1e30)


def kernel(
    n_lat,
    n_lon,
    x,
    g1,
    wqkv,
    table,
    index,
    wproj,
    g2,
    wup,
    wdown,
    gm,
    wmerge,
    out,
    x_v,
    sent,
    frame,
    rs,
    mine,
    g1_v,
    wqkv_v,
    table_v,
    index_v,
    wproj_v,
    g2_v,
    wup_v,
    wdown_v,
    gm_v,
    wmerge_v,
    rem_s,
    packed,
    single,
    raw,
    biasx,
    wq,
    wk,
    wv,
    wp,
    gm_s,
    nrm,
    nw,
    q_s,
    k_s,
    v_s,
    at_s,
    out_v,
    fwd_send,
    fwd_recv,
    ret_send,
    ret_recv,
    table_send,
    table_recv,
    own_sem,
    load_sem,
    out_sem,
):
    batch = x.shape[0]
    lat, lon = lax.axis_index("lat"), lax.axis_index("lon")
    up = lax.rem(lat + n_lat - 1, n_lat)
    down = lax.rem(lat + 1, n_lat)
    west = lax.rem(lon + n_lon - 1, n_lon)
    east = lax.rem(lon + 1, n_lon)
    before = ((lat, west), (up, lon), (up, west))
    after = ((lat, east), (down, lon), (down, east))

    barrier = pltpu.get_barrier_semaphore()
    for peer in before + after:
        pl.semaphore_signal(barrier, inc=1, device_id=peer, device_id_type=MESH)

    loads = [
        pltpu.make_async_copy(src, dst, load_sem.at[i])
        for i, (src, dst) in enumerate(
            (
                (index, index_v),
                (table, table_v),
                (g1, g1_v),
                (wqkv, wqkv_v),
                (wproj, wproj_v),
                (g2, g2_v),
                (wup, wup_v),
                (wdown, wdown_v),
                (gm, gm_v),
                (wmerge, wmerge_v),
            )
        )
    ]
    def x_copy(b):
        return pltpu.make_async_copy(x.at[b], x_v.at[b], own_sem.at[b])

    def fwd_copy(b, i):
        return pltpu.make_async_remote_copy(
            src_ref=sent.at[b, 3 - i],
            dst_ref=frame.at[b, i],
            send_sem=fwd_send.at[b, i - 1],
            recv_sem=fwd_recv.at[b, i - 1],
            device_id=before[i - 1],
            device_id_type=MESH,
        )

    def ret_copy(b, i):
        return pltpu.make_async_remote_copy(
            src_ref=rs.at[b, i],
            dst_ref=mine.at[b, 3 - i],
            send_sem=ret_send.at[b, i - 1],
            recv_sem=ret_recv.at[b, i - 1],
            device_id=after[i - 1],
            device_id_type=MESH,
        )

    for b in range(batch):
        x_copy(b).start()
    for load in loads:
        load.start()

    def stage(b, carry):
        x_copy(b).wait()
        for i in range(4):
            rows, cols = 3 * (i // 2), 6 * (i % 2)
            piece = x_v[b, rows : rows + 3, cols : cols + 6].reshape(18, 8, 192)
            pack(piece, frame.at[b, 0] if i == 3 else sent.at[b, i])
        return carry

    lax.fori_loop(0, batch, stage, 0)
    pl.semaphore_wait(barrier, 6)
    for b in range(batch):
        for i in range(1, 4):
            fwd_copy(b, i).start()

    loads[0].wait()
    loads[1].wait()
    is_last = jnp.where(lat == n_lat - 1, 1, 0)
    prepare_tables(table_v, packed, single)
    rem_s[...] = jnp.zeros_like(rem_s)
    rem_s[:, 0:16] = index_v[:, 128:144]
    pair = lon % 2
    twin = (lat, lon + 1 - 2 * pair)

    def table_copy(part, which):
        piece = raw.at[which, :, pl.ds(48 * part, 48)]
        return pltpu.make_async_remote_copy(
            src_ref=piece,
            dst_ref=piece,
            send_sem=table_send.at[part],
            recv_sem=table_recv.at[part],
            device_id=twin,
            device_id_type=MESH,
        )

    for part in range(3):
        gather_groups(6 * part, 6, pair, index_v, rem_s, packed, single, raw)
        table_copy(part, pair).start()
    finish_bias(pair, is_last, raw, biasx)
    for part in range(3):
        table_copy(part, 1 - pair).wait_recv()
    finish_bias(1 - pair, is_last, raw, biasx)

    for load in loads[2:]:
        load.wait()
    gains = gm_v[...].reshape(1, 768)
    for i in range(4):
        gm_s[i : i + 1, :] = gains[:, 192 * i : 192 * i + 192]
    wq[...] = wqkv_v[:, 0:192]
    wk[...] = wqkv_v[:, 192:384]
    wv[...] = jnp.zeros_like(wv)
    wv[:, 0:192] = wqkv_v[:, 384:576]
    wp[...] = jnp.zeros_like(wp)
    wp[:, 0:192] = wproj_v[...]

    lane192 = lax.broadcasted_iota(I32, (1, 192), 1)
    lane256 = lax.broadcasted_iota(I32, (1, 256), 1)
    key_masks = [jnp.where(lane192 // 32 == h, 1.0, 0.0).astype(BF16) for h in range(HEADS)]
    value_masks = [
        jnp.where((lane256 // 32 == h) & (lane256 < 192) | (lane256 == 192 + h), 1.0, 0.0).astype(BF16)
        for h in range(HEADS)
    ]
    ones_part = jnp.where(lane256 >= 192, V_SCALE, 0.0)
    den_lane = lax.broadcasted_iota(I32, (WIN, 128), 1) // 32

    runs = [
        [slice(start, start + 48) for start in (((3 * (i // 2) + r) * 12 + 6 * (i % 2)) * 8 for r in range(3))]
        for i in range(4)
    ]

    def attend(b, carry):
        for i in range(4):
            if i > 0:
                fwd_copy(b, i).wait_recv()
            tokens = norm(unpack(frame[b, i]), g1_v[...])
            for r in range(3):
                rows = runs[i][r]
                nrm[0, rows, :] = tokens[48 * r : 48 * r + 48, 0:128]
                nrm[1, rows, 0:64] = tokens[48 * r : 48 * r + 48, 128:192]
        for w in range(4):
            first, second = 2 * w + 1, (2 * w + 2) % 8
            for half, width in ((0, 128), (1, 64)):
                part = [nrm[half, pl.ds(level, 72, stride=8), :] for level in (first, second)]
                part = jnp.concatenate(part, axis=0).astype(BF16)
                nw[w * WIN : w * WIN + WIN, 128 * half : 128 * half + width] = part[:, 0:width]
        tokens = nw[...]
        q_s[...] = (dot(tokens, wq[...]) * (LOG2E * 32.0**-0.5)).astype(BF16)
        k_s[...] = dot(tokens, wk[...]).astype(BF16)
        v_s[...] = (dot(tokens, wv[...]) * V_SCALE + ones_part).astype(BF16)
        for w in range(4):
            rows = slice(w * WIN, w * WIN + WIN)
            q, k, v = q_s[rows, :], k_s[rows, :], v_s[rows, :]
            probs = []
            values = []
            for tile in range(4):
                if tile < 3:
                    heads = (2 * tile, 2 * tile + 1)
                    keys = jnp.concatenate([k[0:128] * key_masks[h] for h in heads], axis=0)
                    values += [v[0:128] * value_masks[h] for h in heads]
                    bias = jnp.concatenate([biasx[w, h] for h in heads], axis=1)
                else:
                    keys = jnp.concatenate([k[128:144] * key_masks[h] for h in range(HEADS)], axis=0)
                    values += [v[128:144] * value_masks[h] for h in range(HEADS)]
                    bias = biasx[w, HEADS][:, 0:96]
                probs.append(jnp.exp2(dot_nt(q, keys) + bias).astype(BF16))
            summed = dot(jnp.concatenate(probs, axis=1), jnp.concatenate(values, axis=0))
            left, right = summed[:, 0:128], summed[:, 128:256]
            inverse = 1.0 / right
            left_den = jnp.take_along_axis(inverse, 64 + den_lane, axis=1, mode="promise_in_bounds")
            right_den = jnp.take_along_axis(inverse, 64 + 4 + (den_lane & 1), axis=1, mode="promise_in_bounds")
            at_s[rows, 0:128] = (left * left_den).astype(BF16)
            at_s[rows, 128:192] = (right * right_den)[:, 0:64].astype(BF16)
        projected = dot(at_s[...], wp[...])
        for w in range(4):
            first, second = 2 * w + 1, (2 * w + 2) % 8
            for half in range(2):
                lanes = slice(128 * half, 128 * half + 128)
                nrm[half, pl.ds(first, 72, stride=8), :] = projected[w * WIN : w * WIN + 72, lanes]
                nrm[half, pl.ds(second, 72, stride=8), :] = projected[w * WIN + 72 : w * WIN + 144, lanes]
        for i in range(4):
            added = [
                jnp.concatenate([nrm[0, rows, :], nrm[1, rows, 0:64]], axis=1) for rows in runs[i]
            ]
            total = (unpack(frame[b, i]) + jnp.concatenate(added, axis=0)).astype(BF16).reshape(18, 8, 192)
            pack(total, mine.at[b, 3] if i == 0 else rs.at[b, i])
            if i > 0:
                ret_copy(b, i).start()
        return carry

    lax.fori_loop(0, batch, attend, 0)

    def out_copy(b):
        return pltpu.make_async_copy(out_v.at[b], out.at[b], out_sem.at[b])

    def feed(b, carry):
        for i in range(1, 4):
            ret_copy(b, i).wait_recv()
        flat = jnp.concatenate([unpack(mine[b, i]) for i in range(4)], axis=0)
        normed = norm(flat, g2_v[...]).astype(BF16)
        block = flat
        for j in range(3):
            hidden = jax.nn.gelu(dot(normed, wup_v[:, 256 * j : 256 * j + 256])).astype(BF16)
            block = block + dot_nt(hidden, wdown_v[:, 256 * j : 256 * j + 256])
        block = block.astype(BF16).astype(F32).reshape(2, 2, 3, 3, 2, 8, 192)
        parts = []
        for j in range(2):
            for i in range(2):
                rows = (i, i + 2, i + 4)
                pieces = [block[r // 3, half, r % 3, :, j] for r in rows for half in range(2)]
                parts.append(jnp.concatenate(pieces, axis=0).reshape(144, 192))
        average = sum(jnp.sum(p, -1, keepdims=True) for p in parts) * (1.0 / 768)
        parts = [p - average for p in parts]
        spread = sum(jnp.sum(p * p, -1, keepdims=True) for p in parts) * (1.0 / 768)
        scale = lax.rsqrt(spread + 1e-05)
        merged = jnp.zeros((144, 384), F32)
        for i, p in enumerate(parts):
            normed = (p * scale * gm_s[i : i + 1, :]).astype(BF16)
            merged = merged + dot(normed, wmerge_v[192 * i : 192 * i + 192, :])
        out_v[b] = merged.reshape(3, 6, 8, 384).astype(BF16)
        out_copy(b).start()
        return carry

    lax.fori_loop(0, batch, feed, 0)

    for part in range(3):
        table_copy(part, pair).wait_send()
    for b in range(batch):
        out_copy(b).wait()
        for i in range(1, 4):
            fwd_copy(b, i).wait_send()
            ret_copy(b, i).wait_send()


def body(fields, norm1_gain, w_qkv, earth_bias, bias_index, w_proj, norm2_gain, w_up, w_down, merge_gain, w_merge):
    batch = fields.shape[0]
    args = (
        fields.transpose(0, 2, 3, 1, 4),
        norm1_gain.reshape(1, 192),
        w_qkv,
        earth_bias.transpose(1, 2, 0, 3).reshape(6, 4, 3312),
        bias_index,
        w_proj,
        norm2_gain.reshape(1, 192),
        w_up,
        w_down.T,
        merge_gain,
        w_merge,
    )
    block = (batch, 4, 27, 8, 128)
    shapes = [a.shape for a in args]
    dtypes = [a.dtype for a in args]
    loaded = [pltpu.VMEM(s, d) for s, d in zip(shapes[1:], dtypes[1:])]
    merged = pl.pallas_call(
        functools.partial(kernel, lax.axis_size("lat"), lax.axis_size("lon")),
        out_shape=jax.ShapeDtypeStruct((batch, 3, 6, 8, 384), BF16),
        in_specs=[pl.BlockSpec(memory_space=pl.ANY)] * len(args),
        out_specs=pl.BlockSpec(memory_space=pl.ANY),
        scratch_shapes=[
            pltpu.VMEM((batch, 6, 12, 8, 192), BF16),
            pltpu.VMEM(block, BF16),
            pltpu.VMEM(block, BF16),
            pltpu.VMEM(block, BF16),
            pltpu.VMEM(block, BF16),
            *loaded,
            pltpu.VMEM((WIN, 128), I32),
            pltpu.VMEM((2, 8, 128 * CHUNKS), I32),
            pltpu.VMEM((2, HEADS, 1, 128 * CHUNKS), I32),
            pltpu.VMEM((2, 7, WIN, 128), I32),
            pltpu.VMEM((4, 7, WIN, 128), F32),
            pltpu.VMEM((192, 192), BF16),
            pltpu.VMEM((192, 192), BF16),
            pltpu.VMEM((192, 256), BF16),
            pltpu.VMEM((192, 256), BF16),
            pltpu.VMEM((4, 192), F32),
            pltpu.VMEM((2, 576, 128), F32),
            pltpu.VMEM((576, 192), BF16),
            pltpu.VMEM((576, 192), BF16),
            pltpu.VMEM((576, 192), BF16),
            pltpu.VMEM((576, 256), BF16),
            pltpu.VMEM((576, 192), BF16),
            pltpu.VMEM((batch, 3, 6, 8, 384), BF16),
            pltpu.SemaphoreType.DMA((batch, 3)),
            pltpu.SemaphoreType.DMA((batch, 3)),
            pltpu.SemaphoreType.DMA((batch, 3)),
            pltpu.SemaphoreType.DMA((batch, 3)),
            pltpu.SemaphoreType.DMA((3,)),
            pltpu.SemaphoreType.DMA((3,)),
            pltpu.SemaphoreType.DMA((batch,)),
            pltpu.SemaphoreType.DMA((10,)),
            pltpu.SemaphoreType.DMA((batch,)),
        ],
        compiler_params=pltpu.CompilerParams(
            collective_id=0, has_side_effects=True, vmem_limit_bytes=56 * 1024 * 1024
        ),
    )(*args)
    return merged.transpose(0, 3, 1, 2, 4)


def solution(mesh):
    in_specs = (
        P(None, None, "lat", "lon", None),
        P(),
        P(),
        P(None, "lat", None, None),
        P(),
        P(),
        P(),
        P(),
        P(),
        P(),
        P(),
    )
    out_specs = P(None, None, "lat", "lon", None)
    return jax.shard_map(body, mesh=mesh, in_specs=in_specs, out_specs=out_specs, check_vma=False)
```

```python
import functools

import jax
import jax.numpy as jnp
from jax import lax
from jax.experimental import pallas as pl
from jax.experimental.pallas import tpu as pltpu
from jax.sharding import PartitionSpec as P

MESH = pl.DeviceIdType.MESH
F32 = jnp.float32
BF16 = jnp.bfloat16
I32 = jnp.int32
LOG2E = 1.4426950408889634
FIXED = 4096.0
HEADS = 6
WIN = 144
CHUNKS = 26
V_SCALE = 2.0**-8


def norm(values, gain):
    average = jnp.mean(values, -1, keepdims=True)
    centred = values - average
    spread = jnp.mean(centred * centred, -1, keepdims=True)
    return centred * lax.rsqrt(spread + 1e-05) * gain


def dot(a, b):
    return jnp.dot(a, b, preferred_element_type=F32)


def dot_nt(a, b):
    return lax.dot_general(a, b, (((1,), (1,)), ((), ())), preferred_element_type=F32)


def pack(piece, target):
    target[0:18] = piece[:, :, 0:128]
    target[18:27] = jnp.concatenate([piece[0:9, :, 128:192], piece[9:18, :, 128:192]], axis=2)


def unpack(tiles):
    tiles = tiles.astype(F32)
    last = jnp.concatenate([tiles[18:27, :, 0:64], tiles[18:27, :, 64:128]], axis=0)
    return jnp.concatenate([tiles[0:18], last], axis=2).reshape(144, 192)


def slot_label(slot, level_flag, lat_flag):
    level = jnp.where(slot >= 72, level_flag, 0)
    within = jnp.where(slot >= 72, slot - 72, slot)
    return 2 * level + jnp.where(within >= 36, lat_flag, 0)


def prepare_tables(table_v, packed, single):
    packed[...] = jnp.zeros_like(packed)
    single[...] = jnp.zeros_like(single)
    for head in range(HEADS):
        fixed = jnp.round(table_v[head].astype(F32) * (LOG2E * FIXED)).astype(I32)
        for pair in range(2):
            low = fixed[2 * pair : 2 * pair + 1] & 0xFFFF
            high = fixed[2 * pair + 1 : 2 * pair + 2] << 16
            packed[pair, head : head + 1, 0:3312] = low | high
            single[pair, head, :, 0:3312] = low | high


def gather_groups(first, count, pair, index_v, single, raw):
    def one_group(group, carry):
        start = pl.multiple_of(group * 8, 8)
        index = index_v[pl.ds(start, 8), 0:128]
        high, low = index >> 7, index & 127
        accs = [jnp.zeros((8, 128), I32) for _ in range(HEADS)]
        for chunk in range(CHUNKS):
            here = high == chunk
            for head in range(HEADS):
                source = jnp.broadcast_to(single[pair, head, :, 128 * chunk : 128 * chunk + 128], (8, 128))
                got = jnp.take_along_axis(source, low, axis=1, mode="promise_in_bounds")
                accs[head] = jnp.where(here, got, accs[head])
        for head in range(HEADS):
            raw[pair, head, pl.ds(start, 8), :] = accs[head]
        return carry

    lax.fori_loop(first, first + count, one_group, 0)


def gather_rest(pair, rem_s, packed, raw):
    sub = lax.broadcasted_iota(I32, (8, 128), 0)
    lane = lax.broadcasted_iota(I32, (8, 128), 1)
    turn = ((lane >> 4) - sub) & 7
    back = (lane + 16 * sub) & 127
    groups = [slice(8 * g, 8 * g + 8) for g in range(WIN // 8)]
    for rows in groups:
        placed = pltpu.roll(rem_s[rows, :].astype(F32), 0, 1, stride=16, stride_axis=0)
        rem_s[rows, :] = jnp.broadcast_to(jnp.sum(placed, 0, keepdims=True), (8, 128)).astype(I32)

    def look_up(step, carry):
        for i in range(3):
            start = pl.multiple_of((3 * step + i) * 8, 8)
            rem = rem_s[pl.ds(start, 8), :]
            high, low = rem >> 7, rem & 127
            acc = jnp.zeros((8, 128), I32)
            for chunk in range(CHUNKS):
                source = packed[pair, :, 128 * chunk : 128 * chunk + 128]
                got = jnp.take_along_axis(source, low, axis=1, mode="promise_in_bounds")
                acc = jnp.where(high == chunk, got, acc)
            raw[pair, HEADS, pl.ds(start, 8), :] = acc
        return carry

    lax.fori_loop(0, WIN // 24, look_up, 0)
    for rows in groups:
        acc = pltpu.roll(raw[pair, HEADS, rows, :], 0, 1, stride=16, stride_axis=0)
        acc = jnp.take_along_axis(acc, turn, axis=0, mode="promise_in_bounds")
        raw[pair, HEADS, rows, :] = jnp.take_along_axis(acc, back, axis=1, mode="promise_in_bounds")


def finish_bias(pair, is_last, raw, biasx):
    for rows in range(0, WIN, 48):
        query = lax.broadcasted_iota(I32, (48, 128), 0) + rows
        lane = lax.broadcasted_iota(I32, (48, 128), 1)
        for key, tiles in ((lane, range(HEADS)), (128 + (lane & 15), (HEADS,))):
            for half in range(2):
                level_flag = jnp.where(pair == 1, half, 0)
                same = slot_label(query, level_flag, is_last) == slot_label(key, level_flag, is_last)
                for tile in tiles:
                    value = raw[pair, tile, rows : rows + 48, :]
                    value = (value >> 16) if half else ((value << 16) >> 16)
                    value = value.astype(F32) * (1.0 / FIXED)
                    biasx[2 * pair + half, tile, rows : rows + 48, :] = jnp.where(same, value, -1e30)


def kernel(
    n_lat,
    n_lon,
    x,
    g1,
    wqkv,
    table,
    index,
    wproj,
    g2,
    wup,
    wdown,
    gm,
    wmerge,
    out,
    x_v,
    sent,
    frame,
    rs,
    mine,
    g1_v,
    wqkv_v,
    table_v,
    index_v,
    wproj_v,
    g2_v,
    wup_v,
    wdown_v,
    gm_v,
    wmerge_v,
    rem_s,
    packed,
    single,
    raw,
    biasx,
    wq,
    wk,
    wv,
    wp,
    gm_s,
    nrm,
    nw,
    q_s,
    k_s,
    v_s,
    at_s,
    out_v,
    fwd_send,
    fwd_recv,
    ret_send,
    ret_recv,
    table_send,
    table_recv,
    own_sem,
    load_sem,
    out_sem,
):
    batch = x.shape[0]
    lat, lon = lax.axis_index("lat"), lax.axis_index("lon")
    up = lax.rem(lat + n_lat - 1, n_lat)
    down = lax.rem(lat + 1, n_lat)
    west = lax.rem(lon + n_lon - 1, n_lon)
    east = lax.rem(lon + 1, n_lon)
    before = ((lat, west), (up, lon), (up, west))
    after = ((lat, east), (down, lon), (down, east))

    barrier = pltpu.get_barrier_semaphore()
    for peer in before + after:
        pl.semaphore_signal(barrier, inc=1, device_id=peer, device_id_type=MESH)

    loads = [
        pltpu.make_async_copy(src, dst, load_sem.at[i])
        for i, (src, dst) in enumerate(
            (
                (index, index_v),
                (table, table_v),
                (g1, g1_v),
                (wqkv, wqkv_v),
                (wproj, wproj_v),
                (g2, g2_v),
                (wup, wup_v),
                (wdown, wdown_v),
                (gm, gm_v),
                (wmerge, wmerge_v),
            )
        )
    ]
    def x_copy(b):
        return pltpu.make_async_copy(x.at[b], x_v.at[b], own_sem.at[b])

    def fwd_copy(b, i):
        return pltpu.make_async_remote_copy(
            src_ref=sent.at[b, 3 - i],
            dst_ref=frame.at[b, i],
            send_sem=fwd_send.at[b, i - 1],
            recv_sem=fwd_recv.at[b, i - 1],
            device_id=before[i - 1],
            device_id_type=MESH,
        )

    def ret_copy(b, i):
        return pltpu.make_async_remote_copy(
            src_ref=rs.at[b, i],
            dst_ref=mine.at[b, 3 - i],
            send_sem=ret_send.at[b, i - 1],
            recv_sem=ret_recv.at[b, i - 1],
            device_id=after[i - 1],
            device_id_type=MESH,
        )

    for b in range(batch):
        x_copy(b).start()
    for load in loads:
        load.start()

    def stage(b, carry):
        x_copy(b).wait()
        for i in range(4):
            rows, cols = 3 * (i // 2), 6 * (i % 2)
            piece = x_v[b, rows : rows + 3, cols : cols + 6].reshape(18, 8, 192)
            pack(piece, frame.at[b, 0] if i == 3 else sent.at[b, i])
        return carry

    lax.fori_loop(0, batch, stage, 0)
    pl.semaphore_wait(barrier, 6)
    for b in range(batch):
        for i in range(1, 4):
            fwd_copy(b, i).start()

    loads[0].wait()
    loads[1].wait()
    is_last = jnp.where(lat == n_lat - 1, 1, 0)
    prepare_tables(table_v, packed, single)
    rem_s[...] = jnp.zeros_like(rem_s)
    rem_s[:, 0:16] = index_v[:, 128:144]
    pair = lon % 2
    twin = (lat, lon + 1 - 2 * pair)

    def table_copy(part, which):
        piece = raw.at[which, :, pl.ds(48 * part, 48)]
        return pltpu.make_async_remote_copy(
            src_ref=piece,
            dst_ref=piece,
            send_sem=table_send.at[part],
            recv_sem=table_recv.at[part],
            device_id=twin,
            device_id_type=MESH,
        )

    gather_rest(pair, rem_s, packed, raw)
    for part in range(3):
        gather_groups(6 * part, 6, pair, index_v, single, raw)
        table_copy(part, pair).start()
    finish_bias(pair, is_last, raw, biasx)
    for part in range(3):
        table_copy(part, 1 - pair).wait_recv()
    finish_bias(1 - pair, is_last, raw, biasx)

    for load in loads[2:]:
        load.wait()
    gains = gm_v[...].reshape(1, 768)
    for i in range(4):
        gm_s[i : i + 1, :] = gains[:, 192 * i : 192 * i + 192]
    wq[...] = wqkv_v[:, 0:192]
    wk[...] = wqkv_v[:, 192:384]
    wv[...] = jnp.zeros_like(wv)
    wv[:, 0:192] = wqkv_v[:, 384:576]
    wp[...] = jnp.zeros_like(wp)
    wp[:, 0:192] = wproj_v[...]

    lane192 = lax.broadcasted_iota(I32, (1, 192), 1)
    lane256 = lax.broadcasted_iota(I32, (1, 256), 1)
    key_masks = [jnp.where(lane192 // 32 == h, 1.0, 0.0).astype(BF16) for h in range(HEADS)]
    value_masks = [
        jnp.where((lane256 // 32 == h) & (lane256 < 192) | (lane256 == 192 + h), 1.0, 0.0).astype(BF16)
        for h in range(HEADS)
    ]
    ones_part = jnp.where(lane256 >= 192, V_SCALE, 0.0)
    den_lane = lax.broadcasted_iota(I32, (WIN, 128), 1) // 32

    runs = [
        [slice(start, start + 48) for start in (((3 * (i // 2) + r) * 12 + 6 * (i % 2)) * 8 for r in range(3))]
        for i in range(4)
    ]

    def attend(b, carry):
        for i in range(4):
            if i > 0:
                fwd_copy(b, i).wait_recv()
            tokens = norm(unpack(frame[b, i]), g1_v[...])
            for r in range(3):
                rows = runs[i][r]
                nrm[0, rows, :] = tokens[48 * r : 48 * r + 48, 0:128]
                nrm[1, rows, 0:64] = tokens[48 * r : 48 * r + 48, 128:192]
        for w in range(4):
            first, second = 2 * w + 1, (2 * w + 2) % 8
            for half, width in ((0, 128), (1, 64)):
                part = [nrm[half, pl.ds(level, 72, stride=8), :] for level in (first, second)]
                part = jnp.concatenate(part, axis=0).astype(BF16)
                nw[w * WIN : w * WIN + WIN, 128 * half : 128 * half + width] = part[:, 0:width]
        tokens = nw[...]
        q_s[...] = (dot(tokens, wq[...]) * (LOG2E * 32.0**-0.5)).astype(BF16)
        k_s[...] = dot(tokens, wk[...]).astype(BF16)
        v_s[...] = (dot(tokens, wv[...]) * V_SCALE + ones_part).astype(BF16)
        for w in range(4):
            rows = slice(w * WIN, w * WIN + WIN)
            q, k, v = q_s[rows, :], k_s[rows, :], v_s[rows, :]
            probs = []
            values = []
            for tile in range(4):
                if tile < 3:
                    heads = (2 * tile, 2 * tile + 1)
                    lanes = slice(0, 128) if tile < 2 else slice(128, 192)
                    keys = jnp.concatenate([k[0:128, lanes] * key_masks[h][:, lanes] for h in heads], axis=0)
                    query = q[:, lanes]
                    values += [v[0:128] * value_masks[h] for h in heads]
                    bias = jnp.concatenate([biasx[w, h] for h in heads], axis=1)
                else:
                    query = q
                    keys = jnp.concatenate([k[128:144] * key_masks[h] for h in range(HEADS)], axis=0)
                    values += [v[128:144] * value_masks[h] for h in range(HEADS)]
                    bias = biasx[w, HEADS][:, 0:96]
                probs.append(jnp.exp2(dot_nt(query, keys) + bias).astype(BF16))
            summed = dot(jnp.concatenate(probs, axis=1), jnp.concatenate(values, axis=0))
            left, right = summed[:, 0:128], summed[:, 128:256]
            inverse = 1.0 / right
            left_den = jnp.take_along_axis(inverse, 64 + den_lane, axis=1, mode="promise_in_bounds")
            right_den = jnp.take_along_axis(inverse, 64 + 4 + (den_lane & 1), axis=1, mode="promise_in_bounds")
            at_s[rows, 0:128] = (left * left_den).astype(BF16)
            at_s[rows, 128:192] = (right * right_den)[:, 0:64].astype(BF16)
        projected = dot(at_s[...], wp[...])
        for w in range(4):
            first, second = 2 * w + 1, (2 * w + 2) % 8
            for half in range(2):
                lanes = slice(128 * half, 128 * half + 128)
                nrm[half, pl.ds(first, 72, stride=8), :] = projected[w * WIN : w * WIN + 72, lanes]
                nrm[half, pl.ds(second, 72, stride=8), :] = projected[w * WIN + 72 : w * WIN + 144, lanes]
        for i in range(4):
            added = [
                jnp.concatenate([nrm[0, rows, :], nrm[1, rows, 0:64]], axis=1) for rows in runs[i]
            ]
            total = (unpack(frame[b, i]) + jnp.concatenate(added, axis=0)).astype(BF16).reshape(18, 8, 192)
            pack(total, mine.at[b, 3] if i == 0 else rs.at[b, i])
            if i > 0:
                ret_copy(b, i).start()
        return carry

    lax.fori_loop(0, batch, attend, 0)

    def out_copy(b):
        return pltpu.make_async_copy(out_v.at[b], out.at[b], out_sem.at[b])

    def feed(b, carry):
        for i in range(1, 4):
            ret_copy(b, i).wait_recv()
        flat = jnp.concatenate([unpack(mine[b, i]) for i in range(4)], axis=0)
        normed = norm(flat, g2_v[...]).astype(BF16)
        block = flat
        for j in range(3):
            hidden = jax.nn.gelu(dot(normed, wup_v[:, 256 * j : 256 * j + 256])).astype(BF16)
            block = block + dot_nt(hidden, wdown_v[:, 256 * j : 256 * j + 256])
        block = block.astype(BF16).astype(F32).reshape(2, 2, 3, 3, 2, 8, 192)
        parts = []
        for j in range(2):
            for i in range(2):
                rows = (i, i + 2, i + 4)
                pieces = [block[r // 3, half, r % 3, :, j] for r in rows for half in range(2)]
                parts.append(jnp.concatenate(pieces, axis=0).reshape(144, 192))
        average = sum(jnp.sum(p, -1, keepdims=True) for p in parts) * (1.0 / 768)
        parts = [p - average for p in parts]
        spread = sum(jnp.sum(p * p, -1, keepdims=True) for p in parts) * (1.0 / 768)
        scale = lax.rsqrt(spread + 1e-05)
        merged = jnp.zeros((144, 384), F32)
        for i, p in enumerate(parts):
            normed = (p * scale * gm_s[i : i + 1, :]).astype(BF16)
            merged = merged + dot(normed, wmerge_v[192 * i : 192 * i + 192, :])
        out_v[b] = merged.reshape(3, 6, 8, 384).astype(BF16)
        out_copy(b).start()
        return carry

    lax.fori_loop(0, batch, feed, 0)

    for part in range(3):
        table_copy(part, pair).wait_send()
    for b in range(batch):
        out_copy(b).wait()
        for i in range(1, 4):
            fwd_copy(b, i).wait_send()
            ret_copy(b, i).wait_send()


def body(fields, norm1_gain, w_qkv, earth_bias, bias_index, w_proj, norm2_gain, w_up, w_down, merge_gain, w_merge):
    batch = fields.shape[0]
    args = (
        fields.transpose(0, 2, 3, 1, 4),
        norm1_gain.reshape(1, 192),
        w_qkv,
        earth_bias.transpose(1, 2, 0, 3).reshape(6, 4, 3312),
        bias_index,
        w_proj,
        norm2_gain.reshape(1, 192),
        w_up,
        w_down.T,
        merge_gain,
        w_merge,
    )
    block = (batch, 4, 27, 8, 128)
    shapes = [a.shape for a in args]
    dtypes = [a.dtype for a in args]
    loaded = [pltpu.VMEM(s, d) for s, d in zip(shapes[1:], dtypes[1:])]
    merged = pl.pallas_call(
        functools.partial(kernel, lax.axis_size("lat"), lax.axis_size("lon")),
        out_shape=jax.ShapeDtypeStruct((batch, 3, 6, 8, 384), BF16),
        in_specs=[pl.BlockSpec(memory_space=pl.ANY)] * len(args),
        out_specs=pl.BlockSpec(memory_space=pl.ANY),
        scratch_shapes=[
            pltpu.VMEM((batch, 6, 12, 8, 192), BF16),
            pltpu.VMEM(block, BF16),
            pltpu.VMEM(block, BF16),
            pltpu.VMEM(block, BF16),
            pltpu.VMEM(block, BF16),
            *loaded,
            pltpu.VMEM((WIN, 128), I32),
            pltpu.VMEM((2, 8, 128 * CHUNKS), I32),
            pltpu.VMEM((2, HEADS, 1, 128 * CHUNKS), I32),
            pltpu.VMEM((2, 7, WIN, 128), I32),
            pltpu.VMEM((4, 7, WIN, 128), F32),
            pltpu.VMEM((192, 192), BF16),
            pltpu.VMEM((192, 192), BF16),
            pltpu.VMEM((192, 256), BF16),
            pltpu.VMEM((192, 256), BF16),
            pltpu.VMEM((4, 192), F32),
            pltpu.VMEM((2, 576, 128), F32),
            pltpu.VMEM((576, 192), BF16),
            pltpu.VMEM((576, 192), BF16),
            pltpu.VMEM((576, 192), BF16),
            pltpu.VMEM((576, 256), BF16),
            pltpu.VMEM((576, 192), BF16),
            pltpu.VMEM((batch, 3, 6, 8, 384), BF16),
            pltpu.SemaphoreType.DMA((batch, 3)),
            pltpu.SemaphoreType.DMA((batch, 3)),
            pltpu.SemaphoreType.DMA((batch, 3)),
            pltpu.SemaphoreType.DMA((batch, 3)),
            pltpu.SemaphoreType.DMA((3,)),
            pltpu.SemaphoreType.DMA((3,)),
            pltpu.SemaphoreType.DMA((batch,)),
            pltpu.SemaphoreType.DMA((10,)),
            pltpu.SemaphoreType.DMA((batch,)),
        ],
        compiler_params=pltpu.CompilerParams(
            collective_id=0, has_side_effects=True, vmem_limit_bytes=56 * 1024 * 1024
        ),
    )(*args)
    return merged.transpose(0, 3, 1, 2, 4)


def solution(mesh):
    in_specs = (
        P(None, None, "lat", "lon", None),
        P(),
        P(),
        P(None, "lat", None, None),
        P(),
        P(),
        P(),
        P(),
        P(),
        P(),
        P(),
    )
    out_specs = P(None, None, "lat", "lon", None)
    return jax.shard_map(body, mesh=mesh, in_specs=in_specs, out_specs=out_specs, check_vma=False)
```

```python
import functools

import jax
import jax.numpy as jnp
from jax import lax
from jax.experimental import pallas as pl
from jax.experimental.pallas import tpu as pltpu
from jax.sharding import PartitionSpec as P

MESH = pl.DeviceIdType.MESH
F32 = jnp.float32
BF16 = jnp.bfloat16
I32 = jnp.int32
LOG2E = 1.4426950408889634
FIXED = 4096.0
HEADS = 6
WIN = 144
CHUNKS = 26
V_SCALE = 2.0**-8


def norm(values, gain):
    average = jnp.mean(values, -1, keepdims=True)
    centred = values - average
    spread = jnp.mean(centred * centred, -1, keepdims=True)
    return centred * lax.rsqrt(spread + 1e-05) * gain


def dot(a, b):
    return jnp.dot(a, b, preferred_element_type=F32)


def dot_nt(a, b):
    return lax.dot_general(a, b, (((1,), (1,)), ((), ())), preferred_element_type=F32)


def pack(piece, target):
    target[0:18] = piece[:, :, 0:128]
    target[18:27] = jnp.concatenate([piece[0:9, :, 128:192], piece[9:18, :, 128:192]], axis=2)


def unpack(tiles):
    tiles = tiles.astype(F32)
    last = jnp.concatenate([tiles[18:27, :, 0:64], tiles[18:27, :, 64:128]], axis=0)
    return jnp.concatenate([tiles[0:18], last], axis=2).reshape(144, 192)


def slot_label(slot, level_flag, lat_flag):
    level = jnp.where(slot >= 72, level_flag, 0)
    within = jnp.where(slot >= 72, slot - 72, slot)
    return 2 * level + jnp.where(within >= 36, lat_flag, 0)


def prepare_tables(table_v, packed, single):
    packed[...] = jnp.zeros_like(packed)
    single[...] = jnp.zeros_like(single)
    for head in range(HEADS):
        fixed = jnp.round(table_v[head].astype(F32) * (LOG2E * FIXED)).astype(I32)
        for pair in range(2):
            low = fixed[2 * pair : 2 * pair + 1] & 0xFFFF
            high = fixed[2 * pair + 1 : 2 * pair + 2] << 16
            packed[pair, head : head + 1, 0:3312] = low | high
            single[pair, head, :, 0:3312] = low | high


def gather_groups(first, count, index_v, single, raw):
    def one_group(group, carry):
        start = pl.multiple_of(group * 8, 8)
        index = index_v[pl.ds(start, 8), 0:128]
        high, low = index >> 7, index & 127
        tables = [(pair, head) for pair in range(2) for head in range(HEADS)]
        accs = [jnp.zeros((8, 128), I32) for _ in tables]
        for chunk in range(CHUNKS):
            here = high == chunk
            for i, (pair, head) in enumerate(tables):
                source = jnp.broadcast_to(single[pair, head, :, 128 * chunk : 128 * chunk + 128], (8, 128))
                got = jnp.take_along_axis(source, low, axis=1, mode="promise_in_bounds")
                accs[i] = jnp.where(here, got, accs[i])
        for (pair, head), acc in zip(tables, accs):
            raw[pair, head, pl.ds(start, 8), :] = acc
        return carry

    lax.fori_loop(first, first + count, one_group, 0)


def gather_rest(first, count, rem_s, packed, raw):
    sub = lax.broadcasted_iota(I32, (8, 128), 0)
    lane = lax.broadcasted_iota(I32, (8, 128), 1)
    turn = ((lane >> 4) - sub) & 7
    back = (lane + 16 * sub) & 127
    groups = [pl.ds(pl.multiple_of(8 * (first + g), 8), 8) for g in range(count)]
    for rows in groups:
        placed = pltpu.roll(rem_s[rows, :].astype(F32), 0, 1, stride=16, stride_axis=0)
        rem_s[rows, :] = jnp.broadcast_to(jnp.sum(placed, 0, keepdims=True), (8, 128)).astype(I32)

    def look_up(group, carry):
        rows = pl.ds(pl.multiple_of(group * 8, 8), 8)
        rem = rem_s[rows, :]
        high, low = rem >> 7, rem & 127
        accs = [jnp.zeros((8, 128), I32) for _ in range(2)]
        for chunk in range(CHUNKS):
            here = high == chunk
            for pair in range(2):
                source = packed[pair, :, 128 * chunk : 128 * chunk + 128]
                got = jnp.take_along_axis(source, low, axis=1, mode="promise_in_bounds")
                accs[pair] = jnp.where(here, got, accs[pair])
        for pair in range(2):
            raw[pair, HEADS, rows, :] = accs[pair]
        return carry

    lax.fori_loop(first, first + count, look_up, 0)
    for rows in groups:
        for pair in range(2):
            acc = pltpu.roll(raw[pair, HEADS, rows, :], 0, 1, stride=16, stride_axis=0)
            acc = jnp.take_along_axis(acc, turn, axis=0, mode="promise_in_bounds")
            raw[pair, HEADS, rows, :] = jnp.take_along_axis(acc, back, axis=1, mode="promise_in_bounds")


def finish_bias(first, is_last, raw, biasx):
    def some_rows(step, carry):
        start = pl.multiple_of((first + 3 * step) * 8, 8)
        rows = pl.ds(start, 24)
        query = lax.broadcasted_iota(I32, (24, 128), 0) + start
        lane = lax.broadcasted_iota(I32, (24, 128), 1)
        for key, tiles in ((lane, range(HEADS)), (128 + (lane & 15), (HEADS,))):
            for level_window in range(4):
                if level_window != 1 and level_window != 2:
                    level_flag = 1 if level_window == 3 else 0
                    same = slot_label(query, level_flag, is_last) == slot_label(key, level_flag, is_last)
                    if level_window == 0:
                        plain = same
                keep = same if level_window == 3 else plain
                for tile in tiles:
                    value = raw[level_window // 2, tile, rows, :]
                    value = (value >> 16) if level_window % 2 else ((value << 16) >> 16)
                    value = value.astype(F32) * (1.0 / FIXED)
                    biasx[level_window, tile, rows, :] = jnp.where(keep, value, -1e30)
        return carry

    lax.fori_loop(0, 3, some_rows, 0)


def kernel(
    n_lat,
    n_lon,
    x,
    g1,
    wqkv,
    table,
    index,
    wproj,
    g2,
    wup,
    wdown,
    gm,
    wmerge,
    out,
    x_v,
    sent,
    frame,
    rs,
    mine,
    g1_v,
    wqkv_v,
    table_v,
    index_v,
    wproj_v,
    g2_v,
    wup_v,
    wdown_v,
    gm_v,
    wmerge_v,
    rem_s,
    packed,
    single,
    raw,
    biasx,
    wq,
    wk,
    wv,
    wp,
    gm_s,
    nrm,
    nw,
    q_s,
    k_s,
    v_s,
    at_s,
    out_v,
    fwd_send,
    fwd_recv,
    ret_send,
    ret_recv,
    table_send,
    table_recv,
    own_sem,
    load_sem,
    out_sem,
):
    batch = x.shape[0]
    lat, lon = lax.axis_index("lat"), lax.axis_index("lon")
    up = lax.rem(lat + n_lat - 1, n_lat)
    down = lax.rem(lat + 1, n_lat)
    west = lax.rem(lon + n_lon - 1, n_lon)
    east = lax.rem(lon + 1, n_lon)
    before = ((lat, west), (up, lon), (up, west))
    after = ((lat, east), (down, lon), (down, east))

    barrier = pltpu.get_barrier_semaphore()
    for peer in before + after:
        pl.semaphore_signal(barrier, inc=1, device_id=peer, device_id_type=MESH)

    loads = [
        pltpu.make_async_copy(src, dst, load_sem.at[i])
        for i, (src, dst) in enumerate(
            (
                (index, index_v),
                (table, table_v),
                (g1, g1_v),
                (wqkv, wqkv_v),
                (wproj, wproj_v),
                (g2, g2_v),
                (wup, wup_v),
                (wdown, wdown_v),
                (gm, gm_v),
                (wmerge, wmerge_v),
            )
        )
    ]
    def x_copy(b):
        return pltpu.make_async_copy(x.at[b], x_v.at[b], own_sem.at[b])

    def fwd_copy(b, i):
        return pltpu.make_async_remote_copy(
            src_ref=sent.at[b, 3 - i],
            dst_ref=frame.at[b, i],
            send_sem=fwd_send.at[b, i - 1],
            recv_sem=fwd_recv.at[b, i - 1],
            device_id=before[i - 1],
            device_id_type=MESH,
        )

    def ret_copy(b, i):
        return pltpu.make_async_remote_copy(
            src_ref=rs.at[b, i],
            dst_ref=mine.at[b, 3 - i],
            send_sem=ret_send.at[b, i - 1],
            recv_sem=ret_recv.at[b, i - 1],
            device_id=after[i - 1],
            device_id_type=MESH,
        )

    for b in range(batch):
        x_copy(b).start()
    for load in loads:
        load.start()

    def stage(b, carry):
        x_copy(b).wait()
        for i in range(4):
            rows, cols = 3 * (i // 2), 6 * (i % 2)
            piece = x_v[b, rows : rows + 3, cols : cols + 6].reshape(18, 8, 192)
            pack(piece, frame.at[b, 0] if i == 3 else sent.at[b, i])
        return carry

    lax.fori_loop(0, batch, stage, 0)
    pl.semaphore_wait(barrier, 6)
    for b in range(batch):
        for i in (3, 2, 1):
            fwd_copy(b, i).start()

    loads[0].wait()
    loads[1].wait()
    is_last = jnp.where(lat == n_lat - 1, 1, 0)
    prepare_tables(table_v, packed, single)
    rem_s[...] = jnp.zeros_like(rem_s)
    rem_s[:, 0:16] = index_v[:, 128:144]
    half = lon % 2
    twin = (lat, lon + 1 - 2 * half)

    def table_copy(part, which):
        piece = raw.at[:, :, pl.ds(72 * which + 24 * part, 24)]
        return pltpu.make_async_remote_copy(
            src_ref=piece,
            dst_ref=piece,
            send_sem=table_send.at[part],
            recv_sem=table_recv.at[part],
            device_id=twin,
            device_id_type=MESH,
        )

    gather_rest(9 * half, 9, rem_s, packed, raw)
    for part in range(3):
        gather_groups(9 * half + 3 * part, 3, index_v, single, raw)
        table_copy(part, half).start()
    finish_bias(9 * half, is_last, raw, biasx)
    for part in range(3):
        table_copy(part, 1 - half).wait_recv()
    finish_bias(9 - 9 * half, is_last, raw, biasx)

    for load in loads[2:]:
        load.wait()
    gains = gm_v[...].reshape(1, 768)
    for i in range(4):
        gm_s[i : i + 1, :] = gains[:, 192 * i : 192 * i + 192]
    wq[...] = wqkv_v[:, 0:192]
    wk[...] = wqkv_v[:, 192:384]
    wv[...] = jnp.zeros_like(wv)
    wv[:, 0:192] = wqkv_v[:, 384:576]
    wp[...] = jnp.zeros_like(wp)
    wp[:, 0:192] = wproj_v[...]

    lane192 = lax.broadcasted_iota(I32, (1, 192), 1)
    lane256 = lax.broadcasted_iota(I32, (1, 256), 1)
    key_masks = [jnp.where(lane192 // 32 == h, 1.0, 0.0).astype(BF16) for h in range(HEADS)]
    value_masks = [
        jnp.where((lane256 // 32 == h) & (lane256 < 192) | (lane256 == 192 + h), 1.0, 0.0).astype(BF16)
        for h in range(HEADS)
    ]
    ones_part = jnp.where(lane256 >= 192, V_SCALE, 0.0)
    den_lane = lax.broadcasted_iota(I32, (WIN, 128), 1) // 32

    runs = [
        [slice(start, start + 48) for start in (((3 * (i // 2) + r) * 12 + 6 * (i % 2)) * 8 for r in range(3))]
        for i in range(4)
    ]

    def attend(b, carry):
        for i in range(1, 4):
            fwd_copy(b, i).wait_recv()
        for i in range(4):
            tokens = norm(unpack(frame[b, i]), g1_v[...])
            for r in range(3):
                rows = runs[i][r]
                nrm[0, rows, :] = tokens[48 * r : 48 * r + 48, 0:128]
                nrm[1, rows, 0:64] = tokens[48 * r : 48 * r + 48, 128:192]
        for w in range(4):
            first, second = 2 * w + 1, (2 * w + 2) % 8
            for half, width in ((0, 128), (1, 64)):
                part = [nrm[half, pl.ds(level, 72, stride=8), :] for level in (first, second)]
                part = jnp.concatenate(part, axis=0).astype(BF16)
                nw[w * WIN : w * WIN + WIN, 128 * half : 128 * half + width] = part[:, 0:width]
        tokens = nw[...]
        q_s[...] = (dot(tokens, wq[...]) * (LOG2E * 32.0**-0.5)).astype(BF16)
        k_s[...] = dot(tokens, wk[...]).astype(BF16)
        v_s[...] = (dot(tokens, wv[...]) * V_SCALE + ones_part).astype(BF16)
        for w in range(4):
            rows = slice(w * WIN, w * WIN + WIN)
            q, k, v = q_s[rows, :], k_s[rows, :], v_s[rows, :]
            probs = []
            values = []
            for tile in range(4):
                if tile < 3:
                    heads = (2 * tile, 2 * tile + 1)
                    lanes = slice(0, 128) if tile < 2 else slice(128, 192)
                    keys = jnp.concatenate([k[0:128, lanes] * key_masks[h][:, lanes] for h in heads], axis=0)
                    query = q[:, lanes]
                    values += [v[0:128] * value_masks[h] for h in heads]
                    bias = jnp.concatenate([biasx[w, h] for h in heads], axis=1)
                else:
                    query = q
                    keys = jnp.concatenate([k[128:144] * key_masks[h] for h in range(HEADS)], axis=0)
                    values += [v[128:144] * value_masks[h] for h in range(HEADS)]
                    bias = biasx[w, HEADS][:, 0:96]
                probs.append(jnp.exp2(dot_nt(query, keys) + bias).astype(BF16))
            summed = dot(jnp.concatenate(probs, axis=1), jnp.concatenate(values, axis=0))
            left, right = summed[:, 0:128], summed[:, 128:256]
            inverse = 1.0 / right
            left_den = jnp.take_along_axis(inverse, 64 + den_lane, axis=1, mode="promise_in_bounds")
            right_den = jnp.take_along_axis(inverse, 64 + 4 + (den_lane & 1), axis=1, mode="promise_in_bounds")
            at_s[rows, 0:128] = (left * left_den).astype(BF16)
            at_s[rows, 128:192] = (right * right_den)[:, 0:64].astype(BF16)
        projected = dot(at_s[...], wp[...])
        for w in range(4):
            first, second = 2 * w + 1, (2 * w + 2) % 8
            for half in range(2):
                lanes = slice(128 * half, 128 * half + 128)
                nrm[half, pl.ds(first, 72, stride=8), :] = projected[w * WIN : w * WIN + 72, lanes]
                nrm[half, pl.ds(second, 72, stride=8), :] = projected[w * WIN + 72 : w * WIN + 144, lanes]
        for i in (3, 2, 1, 0):
            added = [
                jnp.concatenate([nrm[0, rows, :], nrm[1, rows, 0:64]], axis=1) for rows in runs[i]
            ]
            total = (unpack(frame[b, i]) + jnp.concatenate(added, axis=0)).astype(BF16).reshape(18, 8, 192)
            pack(total, mine.at[b, 3] if i == 0 else rs.at[b, i])
        for i in (3, 2, 1):
            ret_copy(b, i).start()
        return carry

    lax.fori_loop(0, batch, attend, 0)

    def out_copy(b):
        return pltpu.make_async_copy(out_v.at[b], out.at[b], out_sem.at[b])

    def feed(b, carry):
        for i in range(1, 4):
            ret_copy(b, i).wait_recv()
        flat = jnp.concatenate([unpack(mine[b, i]) for i in range(4)], axis=0)
        normed = norm(flat, g2_v[...]).astype(BF16)
        block = flat
        for j in range(3):
            hidden = jax.nn.gelu(dot(normed, wup_v[:, 256 * j : 256 * j + 256])).astype(BF16)
            block = block + dot_nt(hidden, wdown_v[:, 256 * j : 256 * j + 256])
        block = block.astype(BF16).astype(F32).reshape(2, 2, 3, 3, 2, 8, 192)
        parts = []
        for j in range(2):
            for i in range(2):
                rows = (i, i + 2, i + 4)
                pieces = [block[r // 3, half, r % 3, :, j] for r in rows for half in range(2)]
                parts.append(jnp.concatenate(pieces, axis=0).reshape(144, 192))
        average = sum(jnp.sum(p, -1, keepdims=True) for p in parts) * (1.0 / 768)
        parts = [p - average for p in parts]
        spread = sum(jnp.sum(p * p, -1, keepdims=True) for p in parts) * (1.0 / 768)
        scale = lax.rsqrt(spread + 1e-05)
        merged = jnp.zeros((144, 384), F32)
        for i, p in enumerate(parts):
            normed = (p * scale * gm_s[i : i + 1, :]).astype(BF16)
            merged = merged + dot(normed, wmerge_v[192 * i : 192 * i + 192, :])
        out_v[b] = merged.reshape(3, 6, 8, 384).astype(BF16)
        out_copy(b).start()
        return carry

    lax.fori_loop(0, batch, feed, 0)

    for part in range(3):
        table_copy(part, half).wait_send()
    for b in range(batch):
        out_copy(b).wait()
        for i in range(1, 4):
            fwd_copy(b, i).wait_send()
            ret_copy(b, i).wait_send()


def body(fields, norm1_gain, w_qkv, earth_bias, bias_index, w_proj, norm2_gain, w_up, w_down, merge_gain, w_merge):
    batch = fields.shape[0]
    args = (
        fields.transpose(0, 2, 3, 1, 4),
        norm1_gain.reshape(1, 192),
        w_qkv,
        earth_bias.transpose(1, 2, 0, 3).reshape(6, 4, 3312),
        bias_index,
        w_proj,
        norm2_gain.reshape(1, 192),
        w_up,
        w_down.T,
        merge_gain,
        w_merge,
    )
    block = (batch, 4, 27, 8, 128)
    shapes = [a.shape for a in args]
    dtypes = [a.dtype for a in args]
    loaded = [pltpu.VMEM(s, d) for s, d in zip(shapes[1:], dtypes[1:])]
    merged = pl.pallas_call(
        functools.partial(kernel, lax.axis_size("lat"), lax.axis_size("lon")),
        out_shape=jax.ShapeDtypeStruct((batch, 3, 6, 8, 384), BF16),
        in_specs=[pl.BlockSpec(memory_space=pl.ANY)] * len(args),
        out_specs=pl.BlockSpec(memory_space=pl.ANY),
        scratch_shapes=[
            pltpu.VMEM((batch, 6, 12, 8, 192), BF16),
            pltpu.VMEM(block, BF16),
            pltpu.VMEM(block, BF16),
            pltpu.VMEM(block, BF16),
            pltpu.VMEM(block, BF16),
            *loaded,
            pltpu.VMEM((WIN, 128), I32),
            pltpu.VMEM((2, 8, 128 * CHUNKS), I32),
            pltpu.VMEM((2, HEADS, 1, 128 * CHUNKS), I32),
            pltpu.VMEM((2, 7, WIN, 128), I32),
            pltpu.VMEM((4, 7, WIN, 128), F32),
            pltpu.VMEM((192, 192), BF16),
            pltpu.VMEM((192, 192), BF16),
            pltpu.VMEM((192, 256), BF16),
            pltpu.VMEM((192, 256), BF16),
            pltpu.VMEM((4, 192), F32),
            pltpu.VMEM((2, 576, 128), F32),
            pltpu.VMEM((576, 192), BF16),
            pltpu.VMEM((576, 192), BF16),
            pltpu.VMEM((576, 192), BF16),
            pltpu.VMEM((576, 256), BF16),
            pltpu.VMEM((576, 192), BF16),
            pltpu.VMEM((batch, 3, 6, 8, 384), BF16),
            pltpu.SemaphoreType.DMA((batch, 3)),
            pltpu.SemaphoreType.DMA((batch, 3)),
            pltpu.SemaphoreType.DMA((batch, 3)),
            pltpu.SemaphoreType.DMA((batch, 3)),
            pltpu.SemaphoreType.DMA((3,)),
            pltpu.SemaphoreType.DMA((3,)),
            pltpu.SemaphoreType.DMA((batch,)),
            pltpu.SemaphoreType.DMA((10,)),
            pltpu.SemaphoreType.DMA((batch,)),
        ],
        compiler_params=pltpu.CompilerParams(
            collective_id=0, has_side_effects=True, vmem_limit_bytes=56 * 1024 * 1024
        ),
    )(*args)
    return merged.transpose(0, 3, 1, 2, 4)


def solution(mesh):
    in_specs = (
        P(None, None, "lat", "lon", None),
        P(),
        P(),
        P(None, "lat", None, None),
        P(),
        P(),
        P(),
        P(),
        P(),
        P(),
        P(),
    )
    out_specs = P(None, None, "lat", "lon", None)
    return jax.shard_map(body, mesh=mesh, in_specs=in_specs, out_specs=out_specs, check_vma=False)
```

```python
import functools

import jax
import jax.numpy as jnp
from jax import lax
from jax.experimental import pallas as pl
from jax.experimental.pallas import tpu as pltpu
from jax.sharding import PartitionSpec as P

MESH = pl.DeviceIdType.MESH
F32 = jnp.float32
BF16 = jnp.bfloat16
I32 = jnp.int32
LOG2E = 1.4426950408889634
FIXED = 4096.0
HEADS = 6
WIN = 144
CHUNKS = 26
V_SCALE = 2.0**-8


def norm(values, gain):
    average = jnp.mean(values, -1, keepdims=True)
    centred = values - average
    spread = jnp.mean(centred * centred, -1, keepdims=True)
    return centred * lax.rsqrt(spread + 1e-05) * gain


def dot(a, b):
    return jnp.dot(a, b, preferred_element_type=F32)


def dot_nt(a, b):
    return lax.dot_general(a, b, (((1,), (1,)), ((), ())), preferred_element_type=F32)


def pack(piece, target):
    target[0:18] = piece[:, :, 0:128]
    target[18:27] = jnp.concatenate([piece[0:9, :, 128:192], piece[9:18, :, 128:192]], axis=2)


def unpack(tiles):
    tiles = tiles.astype(F32)
    last = jnp.concatenate([tiles[18:27, :, 0:64], tiles[18:27, :, 64:128]], axis=0)
    return jnp.concatenate([tiles[0:18], last], axis=2).reshape(144, 192)


def slot_label(slot, level_flag, lat_flag):
    level = jnp.where(slot >= 72, level_flag, 0)
    within = jnp.where(slot >= 72, slot - 72, slot)
    return 2 * level + jnp.where(within >= 36, lat_flag, 0)


def prepare_tables(table_v, packed, single):
    packed[...] = jnp.zeros_like(packed)
    single[...] = jnp.zeros_like(single)
    for head in range(HEADS):
        fixed = jnp.round(table_v[head].astype(F32) * (LOG2E * FIXED)).astype(I32)
        for pair in range(2):
            low = fixed[2 * pair : 2 * pair + 1] & 0xFFFF
            high = fixed[2 * pair + 1 : 2 * pair + 2] << 16
            packed[pair, head : head + 1, 0:3312] = low | high
            single[pair, head, :, 0:3312] = low | high


def gather_groups(first, count, index_v, single, raw):
    def one_group(group, carry):
        start = pl.multiple_of(group * 8, 8)
        index = index_v[pl.ds(start, 8), 0:128]
        high, low = index >> 7, index & 127
        tables = [(pair, head) for pair in range(2) for head in range(HEADS)]
        accs = [jnp.zeros((8, 128), I32) for _ in tables]
        for chunk in range(CHUNKS):
            here = high == chunk
            for i, (pair, head) in enumerate(tables):
                source = jnp.broadcast_to(single[pair, head, :, 128 * chunk : 128 * chunk + 128], (8, 128))
                got = jnp.take_along_axis(source, low, axis=1, mode="promise_in_bounds")
                accs[i] = jnp.where(here, got, accs[i])
        for (pair, head), acc in zip(tables, accs):
            raw[pair, head, pl.ds(start, 8), :] = acc
        return carry

    lax.fori_loop(first, first + count, one_group, 0)


def gather_rest(first, count, rem_s, packed, raw):
    sub = lax.broadcasted_iota(I32, (8, 128), 0)
    lane = lax.broadcasted_iota(I32, (8, 128), 1)
    turn = ((lane >> 4) - sub) & 7
    back = (lane + 16 * sub) & 127
    groups = [pl.ds(pl.multiple_of(8 * (first + g), 8), 8) for g in range(count)]
    for rows in groups:
        placed = pltpu.roll(rem_s[rows, :].astype(F32), 0, 1, stride=16, stride_axis=0)
        rem_s[rows, :] = jnp.broadcast_to(jnp.sum(placed, 0, keepdims=True), (8, 128)).astype(I32)

    def look_up(group, carry):
        rows = pl.ds(pl.multiple_of(group * 8, 8), 8)
        rem = rem_s[rows, :]
        high, low = rem >> 7, rem & 127
        accs = [jnp.zeros((8, 128), I32) for _ in range(2)]
        for chunk in range(CHUNKS):
            here = high == chunk
            for pair in range(2):
                source = packed[pair, :, 128 * chunk : 128 * chunk + 128]
                got = jnp.take_along_axis(source, low, axis=1, mode="promise_in_bounds")
                accs[pair] = jnp.where(here, got, accs[pair])
        for pair in range(2):
            raw[pair, HEADS, rows, :] = accs[pair]
        return carry

    lax.fori_loop(first, first + count, look_up, 0)
    for rows in groups:
        for pair in range(2):
            acc = pltpu.roll(raw[pair, HEADS, rows, :], 0, 1, stride=16, stride_axis=0)
            acc = jnp.take_along_axis(acc, turn, axis=0, mode="promise_in_bounds")
            raw[pair, HEADS, rows, :] = jnp.take_along_axis(acc, back, axis=1, mode="promise_in_bounds")


def finish_bias(first, is_last, raw, biasx):
    def some_rows(step, carry):
        start = pl.multiple_of((first + 3 * step) * 8, 8)
        rows = pl.ds(start, 24)
        query = lax.broadcasted_iota(I32, (24, 128), 0) + start
        lane = lax.broadcasted_iota(I32, (24, 128), 1)
        for key, tiles in ((lane, range(HEADS)), (128 + (lane & 15), (HEADS,))):
            for level_window in range(4):
                if level_window != 1 and level_window != 2:
                    level_flag = 1 if level_window == 3 else 0
                    same = slot_label(query, level_flag, is_last) == slot_label(key, level_flag, is_last)
                    if level_window == 0:
                        plain = same
                keep = same if level_window == 3 else plain
                for tile in tiles:
                    value = raw[level_window // 2, tile, rows, :]
                    value = (value >> 16) if level_window % 2 else ((value << 16) >> 16)
                    value = value.astype(F32) * (1.0 / FIXED)
                    biasx[level_window, tile, rows, :] = jnp.where(keep, value, -1e30)
        return carry

    lax.fori_loop(0, 3, some_rows, 0)


def kernel(
    n_lat,
    n_lon,
    x,
    g1,
    wqkv,
    table,
    index,
    wproj,
    g2,
    wup,
    wdown,
    gm,
    wmerge,
    out,
    x_v,
    sent,
    frame,
    rs,
    mine,
    g1_v,
    wqkv_v,
    table_v,
    index_v,
    wproj_v,
    g2_v,
    wup_v,
    wdown_v,
    gm_v,
    wmerge_v,
    rem_s,
    packed,
    single,
    raw,
    biasx,
    wq,
    wk,
    wv,
    wp,
    gm_s,
    nrm,
    nw,
    q_s,
    k_s,
    v_s,
    at_s,
    out_v,
    fwd_send,
    fwd_recv,
    ret_send,
    ret_recv,
    table_send,
    table_recv,
    own_sem,
    load_sem,
    out_sem,
):
    batch = x.shape[0]
    lat, lon = lax.axis_index("lat"), lax.axis_index("lon")
    up = lax.rem(lat + n_lat - 1, n_lat)
    down = lax.rem(lat + 1, n_lat)
    west = lax.rem(lon + n_lon - 1, n_lon)
    east = lax.rem(lon + 1, n_lon)
    before = ((lat, west), (up, lon), (up, west))
    after = ((lat, east), (down, lon), (down, east))

    barrier = pltpu.get_barrier_semaphore()
    for peer in before + after:
        pl.semaphore_signal(barrier, inc=1, device_id=peer, device_id_type=MESH)

    loads = [
        pltpu.make_async_copy(src, dst, load_sem.at[i])
        for i, (src, dst) in enumerate(
            (
                (index, index_v),
                (table, table_v),
                (g1, g1_v),
                (wqkv, wqkv_v),
                (wproj, wproj_v),
                (g2, g2_v),
                (wup, wup_v),
                (wdown, wdown_v),
                (gm, gm_v),
                (wmerge, wmerge_v),
            )
        )
    ]
    def x_copy(b):
        return pltpu.make_async_copy(x.at[b], x_v.at[b], own_sem.at[b])

    def fwd_copy(b, i):
        return pltpu.make_async_remote_copy(
            src_ref=sent.at[b, 3 - i],
            dst_ref=frame.at[b, i],
            send_sem=fwd_send.at[b, i - 1],
            recv_sem=fwd_recv.at[b, i - 1],
            device_id=before[i - 1],
            device_id_type=MESH,
        )

    def ret_copy(b, i):
        return pltpu.make_async_remote_copy(
            src_ref=rs.at[b, i],
            dst_ref=mine.at[b, 3 - i],
            send_sem=ret_send.at[b, i - 1],
            recv_sem=ret_recv.at[b, i - 1],
            device_id=after[i - 1],
            device_id_type=MESH,
        )

    for b in range(batch):
        x_copy(b).start()
    for load in loads:
        load.start()

    def stage(b):
        x_copy(b).wait()
        for i in range(4):
            rows, cols = 3 * (i // 2), 6 * (i % 2)
            piece = x_v[b, rows : rows + 3, cols : cols + 6].reshape(18, 8, 192)
            pack(piece, frame.at[b, 0] if i == 3 else sent.at[b, i])

    for b in range(batch):
        stage(b)
        if b == 0:
            pl.semaphore_wait(barrier, 6)
        for i in (3, 2, 1):
            fwd_copy(b, i).start()

    loads[0].wait()
    loads[1].wait()
    is_last = jnp.where(lat == n_lat - 1, 1, 0)
    prepare_tables(table_v, packed, single)
    rem_s[...] = jnp.zeros_like(rem_s)
    rem_s[:, 0:16] = index_v[:, 128:144]
    half = lon % 2
    twin = (lat, lon + 1 - 2 * half)

    def table_copy(part, which):
        piece = raw.at[:, :, pl.ds(72 * which + 24 * part, 24)]
        return pltpu.make_async_remote_copy(
            src_ref=piece,
            dst_ref=piece,
            send_sem=table_send.at[part],
            recv_sem=table_recv.at[part],
            device_id=twin,
            device_id_type=MESH,
        )

    gather_rest(9 * half, 9, rem_s, packed, raw)
    for part in range(3):
        gather_groups(9 * half + 3 * part, 3, index_v, single, raw)
        table_copy(part, half).start()
    finish_bias(9 * half, is_last, raw, biasx)
    for part in range(3):
        table_copy(part, 1 - half).wait_recv()
    finish_bias(9 - 9 * half, is_last, raw, biasx)

    for load in loads[2:]:
        load.wait()
    gains = gm_v[...].reshape(1, 768)
    for i in range(4):
        gm_s[i : i + 1, :] = gains[:, 192 * i : 192 * i + 192]
    wq[...] = wqkv_v[:, 0:192]
    wk[...] = wqkv_v[:, 192:384]
    wv[...] = jnp.zeros_like(wv)
    wv[:, 0:192] = wqkv_v[:, 384:576]
    wp[...] = jnp.zeros_like(wp)
    wp[:, 0:192] = wproj_v[...]

    lane192 = lax.broadcasted_iota(I32, (1, 192), 1)
    lane256 = lax.broadcasted_iota(I32, (1, 256), 1)
    key_masks = [jnp.where(lane192 // 32 == h, 1.0, 0.0).astype(BF16) for h in range(HEADS)]
    value_masks = [
        jnp.where((lane256 // 32 == h) & (lane256 < 192) | (lane256 == 192 + h), 1.0, 0.0).astype(BF16)
        for h in range(HEADS)
    ]
    ones_part = jnp.where(lane256 >= 192, V_SCALE, 0.0)
    den_lane = lax.broadcasted_iota(I32, (WIN, 128), 1) // 32

    runs = [
        [slice(start, start + 48) for start in (((3 * (i // 2) + r) * 12 + 6 * (i % 2)) * 8 for r in range(3))]
        for i in range(4)
    ]

    def attend(b, carry):
        for i in range(1, 4):
            fwd_copy(b, i).wait_recv()
        for i in range(4):
            tokens = norm(unpack(frame[b, i]), g1_v[...])
            for r in range(3):
                rows = runs[i][r]
                nrm[0, rows, :] = tokens[48 * r : 48 * r + 48, 0:128]
                nrm[1, rows, 0:64] = tokens[48 * r : 48 * r + 48, 128:192]
        for w in range(4):
            first, second = 2 * w + 1, (2 * w + 2) % 8
            for half, width in ((0, 128), (1, 64)):
                part = [nrm[half, pl.ds(level, 72, stride=8), :] for level in (first, second)]
                part = jnp.concatenate(part, axis=0).astype(BF16)
                nw[w * WIN : w * WIN + WIN, 128 * half : 128 * half + width] = part[:, 0:width]
        tokens = nw[...]
        q_s[...] = (dot(tokens, wq[...]) * (LOG2E * 32.0**-0.5)).astype(BF16)
        k_s[...] = dot(tokens, wk[...]).astype(BF16)
        v_s[...] = (dot(tokens, wv[...]) * V_SCALE + ones_part).astype(BF16)
        for w in range(4):
            rows = slice(w * WIN, w * WIN + WIN)
            q, k, v = q_s[rows, :], k_s[rows, :], v_s[rows, :]
            probs = []
            values = []
            for tile in range(4):
                if tile < 3:
                    heads = (2 * tile, 2 * tile + 1)
                    lanes = slice(0, 128) if tile < 2 else slice(128, 192)
                    keys = jnp.concatenate([k[0:128, lanes] * key_masks[h][:, lanes] for h in heads], axis=0)
                    query = q[:, lanes]
                    values += [v[0:128] * value_masks[h] for h in heads]
                    bias = jnp.concatenate([biasx[w, h] for h in heads], axis=1)
                else:
                    query = q
                    keys = jnp.concatenate([k[128:144] * key_masks[h] for h in range(HEADS)], axis=0)
                    values += [v[128:144] * value_masks[h] for h in range(HEADS)]
                    bias = biasx[w, HEADS][:, 0:96]
                probs.append(jnp.exp2(dot_nt(query, keys) + bias).astype(BF16))
            summed = dot(jnp.concatenate(probs, axis=1), jnp.concatenate(values, axis=0))
            left, right = summed[:, 0:128], summed[:, 128:256]
            inverse = 1.0 / right
            left_den = jnp.take_along_axis(inverse, 64 + den_lane, axis=1, mode="promise_in_bounds")
            right_den = jnp.take_along_axis(inverse, 64 + 4 + (den_lane & 1), axis=1, mode="promise_in_bounds")
            at_s[rows, 0:128] = (left * left_den).astype(BF16)
            at_s[rows, 128:192] = (right * right_den)[:, 0:64].astype(BF16)
        projected = dot(at_s[...], wp[...])
        for w in range(4):
            first, second = 2 * w + 1, (2 * w + 2) % 8
            for half in range(2):
                lanes = slice(128 * half, 128 * half + 128)
                nrm[half, pl.ds(first, 72, stride=8), :] = projected[w * WIN : w * WIN + 72, lanes]
                nrm[half, pl.ds(second, 72, stride=8), :] = projected[w * WIN + 72 : w * WIN + 144, lanes]
        for i in (3, 2, 1, 0):
            added = [
                jnp.concatenate([nrm[0, rows, :], nrm[1, rows, 0:64]], axis=1) for rows in runs[i]
            ]
            total = (unpack(frame[b, i]) + jnp.concatenate(added, axis=0)).astype(BF16).reshape(18, 8, 192)
            pack(total, mine.at[b, 3] if i == 0 else rs.at[b, i])
        for i in (3, 2, 1):
            ret_copy(b, i).start()
        return carry

    lax.fori_loop(0, batch, attend, 0)

    def out_copy(b):
        return pltpu.make_async_copy(out_v.at[b], out.at[b], out_sem.at[b])

    def feed(b, carry):
        for i in range(1, 4):
            ret_copy(b, i).wait_recv()
        flat = jnp.concatenate([unpack(mine[b, i]) for i in range(4)], axis=0)
        normed = norm(flat, g2_v[...]).astype(BF16)
        block = flat
        for j in range(3):
            hidden = jax.nn.gelu(dot(normed, wup_v[:, 256 * j : 256 * j + 256])).astype(BF16)
            block = block + dot_nt(hidden, wdown_v[:, 256 * j : 256 * j + 256])
        block = block.astype(BF16).astype(F32).reshape(2, 2, 3, 3, 2, 8, 192)
        parts = []
        for j in range(2):
            for i in range(2):
                rows = (i, i + 2, i + 4)
                pieces = [block[r // 3, half, r % 3, :, j] for r in rows for half in range(2)]
                parts.append(jnp.concatenate(pieces, axis=0).reshape(144, 192))
        average = sum(jnp.sum(p, -1, keepdims=True) for p in parts) * (1.0 / 768)
        parts = [p - average for p in parts]
        spread = sum(jnp.sum(p * p, -1, keepdims=True) for p in parts) * (1.0 / 768)
        scale = lax.rsqrt(spread + 1e-05)
        merged = jnp.zeros((144, 384), F32)
        for i, p in enumerate(parts):
            normed = (p * scale * gm_s[i : i + 1, :]).astype(BF16)
            merged = merged + dot(normed, wmerge_v[192 * i : 192 * i + 192, :])
        out_v[b] = merged.reshape(3, 6, 8, 384).astype(BF16)
        out_copy(b).start()
        return carry

    lax.fori_loop(0, batch, feed, 0)

    for part in range(3):
        table_copy(part, half).wait_send()
    for b in range(batch):
        out_copy(b).wait()
        for i in range(1, 4):
            fwd_copy(b, i).wait_send()
            ret_copy(b, i).wait_send()


def body(fields, norm1_gain, w_qkv, earth_bias, bias_index, w_proj, norm2_gain, w_up, w_down, merge_gain, w_merge):
    batch = fields.shape[0]
    args = (
        fields.transpose(0, 2, 3, 1, 4),
        norm1_gain.reshape(1, 192),
        w_qkv,
        earth_bias.transpose(1, 2, 0, 3).reshape(6, 4, 3312),
        bias_index,
        w_proj,
        norm2_gain.reshape(1, 192),
        w_up,
        w_down.T,
        merge_gain,
        w_merge,
    )
    block = (batch, 4, 27, 8, 128)
    shapes = [a.shape for a in args]
    dtypes = [a.dtype for a in args]
    loaded = [pltpu.VMEM(s, d) for s, d in zip(shapes[1:], dtypes[1:])]
    merged = pl.pallas_call(
        functools.partial(kernel, lax.axis_size("lat"), lax.axis_size("lon")),
        out_shape=jax.ShapeDtypeStruct((batch, 3, 6, 8, 384), BF16),
        in_specs=[pl.BlockSpec(memory_space=pl.ANY)] * len(args),
        out_specs=pl.BlockSpec(memory_space=pl.ANY),
        scratch_shapes=[
            pltpu.VMEM((batch, 6, 12, 8, 192), BF16),
            pltpu.VMEM(block, BF16),
            pltpu.VMEM(block, BF16),
            pltpu.VMEM(block, BF16),
            pltpu.VMEM(block, BF16),
            *loaded,
            pltpu.VMEM((WIN, 128), I32),
            pltpu.VMEM((2, 8, 128 * CHUNKS), I32),
            pltpu.VMEM((2, HEADS, 1, 128 * CHUNKS), I32),
            pltpu.VMEM((2, 7, WIN, 128), I32),
            pltpu.VMEM((4, 7, WIN, 128), F32),
            pltpu.VMEM((192, 192), BF16),
            pltpu.VMEM((192, 192), BF16),
            pltpu.VMEM((192, 256), BF16),
            pltpu.VMEM((192, 256), BF16),
            pltpu.VMEM((4, 192), F32),
            pltpu.VMEM((2, 576, 128), F32),
            pltpu.VMEM((576, 192), BF16),
            pltpu.VMEM((576, 192), BF16),
            pltpu.VMEM((576, 192), BF16),
            pltpu.VMEM((576, 256), BF16),
            pltpu.VMEM((576, 192), BF16),
            pltpu.VMEM((batch, 3, 6, 8, 384), BF16),
            pltpu.SemaphoreType.DMA((batch, 3)),
            pltpu.SemaphoreType.DMA((batch, 3)),
            pltpu.SemaphoreType.DMA((batch, 3)),
            pltpu.SemaphoreType.DMA((batch, 3)),
            pltpu.SemaphoreType.DMA((3,)),
            pltpu.SemaphoreType.DMA((3,)),
            pltpu.SemaphoreType.DMA((batch,)),
            pltpu.SemaphoreType.DMA((10,)),
            pltpu.SemaphoreType.DMA((batch,)),
        ],
        compiler_params=pltpu.CompilerParams(
            collective_id=0, has_side_effects=True, vmem_limit_bytes=56 * 1024 * 1024
        ),
    )(*args)
    return merged.transpose(0, 3, 1, 2, 4)


def solution(mesh):
    in_specs = (
        P(None, None, "lat", "lon", None),
        P(),
        P(),
        P(None, "lat", None, None),
        P(),
        P(),
        P(),
        P(),
        P(),
        P(),
        P(),
    )
    out_specs = P(None, None, "lat", "lon", None)
    return jax.shard_map(body, mesh=mesh, in_specs=in_specs, out_specs=out_specs, check_vma=False)
```

```python
import functools

import jax
import jax.numpy as jnp
from jax import lax
from jax.experimental import pallas as pl
from jax.experimental.pallas import tpu as pltpu
from jax.sharding import PartitionSpec as P

MESH = pl.DeviceIdType.MESH
F32 = jnp.float32
BF16 = jnp.bfloat16
I32 = jnp.int32
LOG2E = 1.4426950408889634
FIXED = 4096.0
HEADS = 6
WIN = 144
CHUNKS = 26
V_SCALE = 2.0**-8


def norm(values, gain):
    average = jnp.mean(values, -1, keepdims=True)
    centred = values - average
    spread = jnp.mean(centred * centred, -1, keepdims=True)
    return centred * lax.rsqrt(spread + 1e-05) * gain


def dot(a, b):
    return jnp.dot(a, b, preferred_element_type=F32)


def dot_nt(a, b):
    return lax.dot_general(a, b, (((1,), (1,)), ((), ())), preferred_element_type=F32)


def pack(piece, target):
    target[0:18] = piece[:, :, 0:128]
    target[18:27] = jnp.concatenate([piece[0:9, :, 128:192], piece[9:18, :, 128:192]], axis=2)


def unpack(tiles):
    tiles = tiles.astype(F32)
    last = jnp.concatenate([tiles[18:27, :, 0:64], tiles[18:27, :, 64:128]], axis=0)
    return jnp.concatenate([tiles[0:18], last], axis=2).reshape(144, 192)


def slot_label(slot, level_flag, lat_flag):
    level = jnp.where(slot >= 72, level_flag, 0)
    within = jnp.where(slot >= 72, slot - 72, slot)
    return 2 * level + jnp.where(within >= 36, lat_flag, 0)


def prepare_tables(table_v, packed, single):
    packed[...] = jnp.zeros_like(packed)
    single[...] = jnp.zeros_like(single)
    for head in range(HEADS):
        fixed = jnp.round(table_v[head].astype(F32) * (LOG2E * FIXED)).astype(I32)
        for pair in range(2):
            low = fixed[2 * pair : 2 * pair + 1] & 0xFFFF
            high = fixed[2 * pair + 1 : 2 * pair + 2] << 16
            packed[pair, head : head + 1, 0:3312] = low | high
            single[pair, head, :, 0:3312] = low | high


def gather_groups(first, count, index_v, single, raw):
    def one_group(group, carry):
        start = pl.multiple_of(group * 8, 8)
        index = index_v[pl.ds(start, 8), 0:128]
        high, low = index >> 7, index & 127
        tables = [(pair, head) for pair in range(2) for head in range(HEADS)]
        accs = [jnp.zeros((8, 128), I32) for _ in tables]
        for chunk in range(CHUNKS):
            here = high == chunk
            for i, (pair, head) in enumerate(tables):
                source = jnp.broadcast_to(single[pair, head, :, 128 * chunk : 128 * chunk + 128], (8, 128))
                got = jnp.take_along_axis(source, low, axis=1, mode="promise_in_bounds")
                accs[i] = jnp.where(here, got, accs[i])
        for (pair, head), acc in zip(tables, accs):
            raw[pair, head, pl.ds(start, 8), :] = acc
        return carry

    lax.fori_loop(first, first + count, one_group, 0)


def gather_rest(first, count, rem_s, packed, raw):
    sub = lax.broadcasted_iota(I32, (8, 128), 0)
    lane = lax.broadcasted_iota(I32, (8, 128), 1)
    turn = ((lane >> 4) - sub) & 7
    back = (lane + 16 * sub) & 127
    groups = [pl.ds(pl.multiple_of(8 * (first + g), 8), 8) for g in range(count)]
    for rows in groups:
        placed = pltpu.roll(rem_s[rows, :].astype(F32), 0, 1, stride=16, stride_axis=0)
        rem_s[rows, :] = jnp.broadcast_to(jnp.sum(placed, 0, keepdims=True), (8, 128)).astype(I32)

    def look_up(group, carry):
        rows = pl.ds(pl.multiple_of(group * 8, 8), 8)
        rem = rem_s[rows, :]
        high, low = rem >> 7, rem & 127
        accs = [jnp.zeros((8, 128), I32) for _ in range(2)]
        for chunk in range(CHUNKS):
            here = high == chunk
            for pair in range(2):
                source = packed[pair, :, 128 * chunk : 128 * chunk + 128]
                got = jnp.take_along_axis(source, low, axis=1, mode="promise_in_bounds")
                accs[pair] = jnp.where(here, got, accs[pair])
        for pair in range(2):
            raw[pair, HEADS, rows, :] = accs[pair]
        return carry

    lax.fori_loop(first, first + count, look_up, 0)
    for rows in groups:
        for pair in range(2):
            acc = pltpu.roll(raw[pair, HEADS, rows, :], 0, 1, stride=16, stride_axis=0)
            acc = jnp.take_along_axis(acc, turn, axis=0, mode="promise_in_bounds")
            raw[pair, HEADS, rows, :] = jnp.take_along_axis(acc, back, axis=1, mode="promise_in_bounds")


def finish_bias(first, is_last, raw, biasx):
    def some_rows(step, carry):
        start = pl.multiple_of((first + 3 * step) * 8, 8)
        rows = pl.ds(start, 24)
        query = lax.broadcasted_iota(I32, (24, 128), 0) + start
        lane = lax.broadcasted_iota(I32, (24, 128), 1)
        for key, tiles in ((lane, range(HEADS)), (128 + (lane & 15), (HEADS,))):
            for level_window in range(4):
                if level_window != 1 and level_window != 2:
                    level_flag = 1 if level_window == 3 else 0
                    same = slot_label(query, level_flag, is_last) == slot_label(key, level_flag, is_last)
                    if level_window == 0:
                        plain = same
                keep = same if level_window == 3 else plain
                for tile in tiles:
                    value = raw[level_window // 2, tile, rows, :]
                    value = (value >> 16) if level_window % 2 else ((value << 16) >> 16)
                    value = value.astype(F32) * (1.0 / FIXED)
                    biasx[level_window, tile, rows, :] = jnp.where(keep, value, -1e30)
        return carry

    lax.fori_loop(0, 3, some_rows, 0)


def kernel(
    n_lat,
    n_lon,
    x,
    g1,
    wqkv,
    table,
    index,
    wproj,
    g2,
    wup,
    wdown,
    gm,
    wmerge,
    out,
    x_v,
    sent,
    frame,
    rs,
    mine,
    g1_v,
    wqkv_v,
    table_v,
    index_v,
    wproj_v,
    g2_v,
    wup_v,
    wdown_v,
    gm_v,
    wmerge_v,
    rem_s,
    packed,
    single,
    raw,
    biasx,
    wq,
    wk,
    wv,
    wp,
    gm_s,
    nrm,
    nw,
    q_s,
    k_s,
    v_s,
    at_s,
    out_v,
    fwd_send,
    fwd_recv,
    ret_send,
    ret_recv,
    table_send,
    table_recv,
    own_sem,
    load_sem,
    out_sem,
):
    batch = x.shape[0]
    lat, lon = lax.axis_index("lat"), lax.axis_index("lon")
    up = lax.rem(lat + n_lat - 1, n_lat)
    down = lax.rem(lat + 1, n_lat)
    west = lax.rem(lon + n_lon - 1, n_lon)
    east = lax.rem(lon + 1, n_lon)
    before = ((lat, west), (up, lon), (up, west))
    after = ((lat, east), (down, lon), (down, east))

    barrier = pltpu.get_barrier_semaphore()
    for peer in before + after:
        pl.semaphore_signal(barrier, inc=1, device_id=peer, device_id_type=MESH)

    loads = [
        pltpu.make_async_copy(src, dst, load_sem.at[i])
        for i, (src, dst) in enumerate(
            (
                (index, index_v),
                (table, table_v),
                (g1, g1_v),
                (wqkv, wqkv_v),
                (wproj, wproj_v),
                (g2, g2_v),
                (wup, wup_v),
                (wdown, wdown_v),
                (gm, gm_v),
                (wmerge, wmerge_v),
            )
        )
    ]
    def x_copy(b):
        return pltpu.make_async_copy(x.at[b], x_v.at[b], own_sem.at[b])

    def fwd_copy(b, i):
        return pltpu.make_async_remote_copy(
            src_ref=sent.at[b, 3 - i],
            dst_ref=frame.at[b, i],
            send_sem=fwd_send.at[b, i - 1],
            recv_sem=fwd_recv.at[b, i - 1],
            device_id=before[i - 1],
            device_id_type=MESH,
        )

    def ret_copy(b, i):
        return pltpu.make_async_remote_copy(
            src_ref=rs.at[b, i],
            dst_ref=mine.at[b, 3 - i],
            send_sem=ret_send.at[b, i - 1],
            recv_sem=ret_recv.at[b, i - 1],
            device_id=after[i - 1],
            device_id_type=MESH,
        )

    for b in range(batch):
        x_copy(b).start()
    for load in loads:
        load.start()

    def stage(b):
        x_copy(b).wait()
        for i in range(4):
            rows, cols = 3 * (i // 2), 6 * (i % 2)
            piece = x_v[b, rows : rows + 3, cols : cols + 6].reshape(18, 8, 192)
            pack(piece, frame.at[b, 0] if i == 3 else sent.at[b, i])

    for b in range(batch):
        stage(b)
        if b == 0:
            pl.semaphore_wait(barrier, 6)
        for i in (3, 2, 1):
            fwd_copy(b, i).start()

    loads[0].wait()
    loads[1].wait()
    is_last = jnp.where(lat == n_lat - 1, 1, 0)
    prepare_tables(table_v, packed, single)
    rem_s[...] = jnp.zeros_like(rem_s)
    rem_s[:, 0:16] = index_v[:, 128:144]
    half = lon % 2
    twin = (lat, lon + 1 - 2 * half)

    def table_copy(part, which):
        piece = raw.at[:, :, pl.ds(72 * which + 24 * part, 24)]
        return pltpu.make_async_remote_copy(
            src_ref=piece,
            dst_ref=piece,
            send_sem=table_send.at[part],
            recv_sem=table_recv.at[part],
            device_id=twin,
            device_id_type=MESH,
        )

    gather_rest(9 * half, 9, rem_s, packed, raw)
    for part in range(3):
        gather_groups(9 * half + 3 * part, 3, index_v, single, raw)
        table_copy(part, half).start()
    finish_bias(9 * half, is_last, raw, biasx)
    for part in range(3):
        table_copy(part, 1 - half).wait_recv()
    finish_bias(9 - 9 * half, is_last, raw, biasx)

    for load in loads[2:]:
        load.wait()
    gains = gm_v[...].reshape(1, 768)
    for i in range(4):
        gm_s[i : i + 1, :] = gains[:, 192 * i : 192 * i + 192]
    wq[...] = wqkv_v[:, 0:192]
    wk[...] = wqkv_v[:, 192:384]
    wv[...] = jnp.zeros_like(wv)
    wv[:, 0:192] = wqkv_v[:, 384:576]
    wp[...] = jnp.zeros_like(wp)
    wp[:, 0:192] = wproj_v[...]

    lane192 = lax.broadcasted_iota(I32, (1, 192), 1)
    lane256 = lax.broadcasted_iota(I32, (1, 256), 1)
    key_masks = [jnp.where(lane192 // 32 == h, 1.0, 0.0).astype(BF16) for h in range(HEADS)]
    value_masks = [
        jnp.where((lane256 // 32 == h) & (lane256 < 192) | (lane256 == 192 + h), 1.0, 0.0).astype(BF16)
        for h in range(HEADS)
    ]
    ones_part = jnp.where(lane256 >= 192, V_SCALE, 0.0)
    den_lane = lax.broadcasted_iota(I32, (WIN, 128), 1) // 32

    runs = [
        [slice(start, start + 48) for start in (((3 * (i // 2) + r) * 12 + 6 * (i % 2)) * 8 for r in range(3))]
        for i in range(4)
    ]

    def attend(b, carry):
        for i in range(1, 4):
            fwd_copy(b, i).wait_recv()
        for i in range(4):
            tokens = norm(unpack(frame[b, i]), g1_v[...])
            for r in range(3):
                rows = runs[i][r]
                nrm[0, rows, :] = tokens[48 * r : 48 * r + 48, 0:128]
                nrm[1, rows, 0:64] = tokens[48 * r : 48 * r + 48, 128:192]
        for w in range(4):
            first, second = 2 * w + 1, (2 * w + 2) % 8
            for half, width in ((0, 128), (1, 64)):
                part = [nrm[half, pl.ds(level, 72, stride=8), :] for level in (first, second)]
                part = jnp.concatenate(part, axis=0).astype(BF16)
                nw[w * WIN : w * WIN + WIN, 128 * half : 128 * half + width] = part[:, 0:width]
        tokens = nw[...]
        q_s[...] = (dot(tokens, wq[...]) * (LOG2E * 32.0**-0.5)).astype(BF16)
        k_s[...] = dot(tokens, wk[...]).astype(BF16)
        v_s[...] = (dot(tokens, wv[...]) * V_SCALE + ones_part).astype(BF16)
        for w in range(4):
            rows = slice(w * WIN, w * WIN + WIN)
            q, k, v = q_s[rows, :], k_s[rows, :], v_s[rows, :]
            probs = []
            values = []
            for tile in range(4):
                if tile < 3:
                    heads = (2 * tile, 2 * tile + 1)
                    lanes = slice(0, 128) if tile < 2 else slice(128, 192)
                    keys = jnp.concatenate([k[0:128, lanes] * key_masks[h][:, lanes] for h in heads], axis=0)
                    query = q[:, lanes]
                    values += [v[0:128] * value_masks[h] for h in heads]
                    bias = jnp.concatenate([biasx[w, h] for h in heads], axis=1)
                else:
                    query = q
                    keys = jnp.concatenate([k[128:144] * key_masks[h] for h in range(HEADS)], axis=0)
                    values += [v[128:144] * value_masks[h] for h in range(HEADS)]
                    bias = biasx[w, HEADS][:, 0:96]
                probs.append(jnp.exp2(dot_nt(query, keys) + bias).astype(BF16))
            summed = dot(jnp.concatenate(probs, axis=1), jnp.concatenate(values, axis=0))
            left, right = summed[:, 0:128], summed[:, 128:256]
            inverse = 1.0 / right
            left_den = jnp.take_along_axis(inverse, 64 + den_lane, axis=1, mode="promise_in_bounds")
            right_den = jnp.take_along_axis(inverse, 64 + 4 + (den_lane & 1), axis=1, mode="promise_in_bounds")
            at_s[rows, 0:128] = (left * left_den).astype(BF16)
            at_s[rows, 128:192] = (right * right_den)[:, 0:64].astype(BF16)
        projected = dot(at_s[...], wp[...])
        for w in range(4):
            first, second = 2 * w + 1, (2 * w + 2) % 8
            for half in range(2):
                lanes = slice(128 * half, 128 * half + 128)
                nrm[half, pl.ds(first, 72, stride=8), :] = projected[w * WIN : w * WIN + 72, lanes]
                nrm[half, pl.ds(second, 72, stride=8), :] = projected[w * WIN + 72 : w * WIN + 144, lanes]
        for i in (3, 2, 1, 0):
            added = [
                jnp.concatenate([nrm[0, rows, :], nrm[1, rows, 0:64]], axis=1) for rows in runs[i]
            ]
            total = (unpack(frame[b, i]) + jnp.concatenate(added, axis=0)).astype(BF16).reshape(18, 8, 192)
            pack(total, mine.at[b, 3] if i == 0 else rs.at[b, i])
        for i in (3, 2, 1):
            ret_copy(b, i).start()
        return carry

    lax.fori_loop(0, batch, attend, 0)

    def out_copy(b):
        return pltpu.make_async_copy(out_v.at[b], out.at[b], out_sem.at[b])

    def feed(batches):
        count = len(batches)
        for b in batches:
            for i in range(1, 4):
                ret_copy(b, i).wait_recv()
        flat = jnp.concatenate([unpack(mine[b, i]) for b in batches for i in range(4)], axis=0)
        normed = norm(flat, g2_v[...]).astype(BF16)
        block = flat
        for j in range(3):
            hidden = jax.nn.gelu(dot(normed, wup_v[:, 256 * j : 256 * j + 256])).astype(BF16)
            block = block + dot_nt(hidden, wdown_v[:, 256 * j : 256 * j + 256])
        block = block.astype(BF16).astype(F32).reshape(count, 2, 2, 3, 3, 2, 8, 192)
        parts = []
        for j in range(2):
            for i in range(2):
                rows = (i, i + 2, i + 4)
                pieces = [block[n, r // 3, half, r % 3, :, j] for n in range(count) for r in rows for half in range(2)]
                parts.append(jnp.concatenate(pieces, axis=0).reshape(144 * count, 192))
        average = sum(jnp.sum(p, -1, keepdims=True) for p in parts) * (1.0 / 768)
        parts = [p - average for p in parts]
        spread = sum(jnp.sum(p * p, -1, keepdims=True) for p in parts) * (1.0 / 768)
        scale = lax.rsqrt(spread + 1e-05)
        merged = jnp.zeros((144 * count, 384), F32)
        for i, p in enumerate(parts):
            normed = (p * scale * gm_s[i : i + 1, :]).astype(BF16)
            merged = merged + dot(normed, wmerge_v[192 * i : 192 * i + 192, :])
        for n, b in enumerate(batches):
            out_v[b] = merged[144 * n : 144 * n + 144].reshape(3, 6, 8, 384).astype(BF16)
            out_copy(b).start()

    def feed_one(b, carry):
        feed([b])
        return carry

    paired = 2 if batch > 2 else 0
    if paired:
        feed([0, 1])
    lax.fori_loop(paired, batch, feed_one, 0)

    for part in range(3):
        table_copy(part, half).wait_send()
    for b in range(batch):
        out_copy(b).wait()
        for i in range(1, 4):
            fwd_copy(b, i).wait_send()
            ret_copy(b, i).wait_send()


def body(fields, norm1_gain, w_qkv, earth_bias, bias_index, w_proj, norm2_gain, w_up, w_down, merge_gain, w_merge):
    batch = fields.shape[0]
    args = (
        fields.transpose(0, 2, 3, 1, 4),
        norm1_gain.reshape(1, 192),
        w_qkv,
        earth_bias.transpose(1, 2, 0, 3).reshape(6, 4, 3312),
        bias_index,
        w_proj,
        norm2_gain.reshape(1, 192),
        w_up,
        w_down.T,
        merge_gain,
        w_merge,
    )
    block = (batch, 4, 27, 8, 128)
    shapes = [a.shape for a in args]
    dtypes = [a.dtype for a in args]
    loaded = [pltpu.VMEM(s, d) for s, d in zip(shapes[1:], dtypes[1:])]
    merged = pl.pallas_call(
        functools.partial(kernel, lax.axis_size("lat"), lax.axis_size("lon")),
        out_shape=jax.ShapeDtypeStruct((batch, 3, 6, 8, 384), BF16),
        in_specs=[pl.BlockSpec(memory_space=pl.ANY)] * len(args),
        out_specs=pl.BlockSpec(memory_space=pl.ANY),
        scratch_shapes=[
            pltpu.VMEM((batch, 6, 12, 8, 192), BF16),
            pltpu.VMEM(block, BF16),
            pltpu.VMEM(block, BF16),
            pltpu.VMEM(block, BF16),
            pltpu.VMEM(block, BF16),
            *loaded,
            pltpu.VMEM((WIN, 128), I32),
            pltpu.VMEM((2, 8, 128 * CHUNKS), I32),
            pltpu.VMEM((2, HEADS, 1, 128 * CHUNKS), I32),
            pltpu.VMEM((2, 7, WIN, 128), I32),
            pltpu.VMEM((4, 7, WIN, 128), F32),
            pltpu.VMEM((192, 192), BF16),
            pltpu.VMEM((192, 192), BF16),
            pltpu.VMEM((192, 256), BF16),
            pltpu.VMEM((192, 256), BF16),
            pltpu.VMEM((4, 192), F32),
            pltpu.VMEM((2, 576, 128), F32),
            pltpu.VMEM((576, 192), BF16),
            pltpu.VMEM((576, 192), BF16),
            pltpu.VMEM((576, 192), BF16),
            pltpu.VMEM((576, 256), BF16),
            pltpu.VMEM((576, 192), BF16),
            pltpu.VMEM((batch, 3, 6, 8, 384), BF16),
            pltpu.SemaphoreType.DMA((batch, 3)),
            pltpu.SemaphoreType.DMA((batch, 3)),
            pltpu.SemaphoreType.DMA((batch, 3)),
            pltpu.SemaphoreType.DMA((batch, 3)),
            pltpu.SemaphoreType.DMA((3,)),
            pltpu.SemaphoreType.DMA((3,)),
            pltpu.SemaphoreType.DMA((batch,)),
            pltpu.SemaphoreType.DMA((10,)),
            pltpu.SemaphoreType.DMA((batch,)),
        ],
        compiler_params=pltpu.CompilerParams(
            collective_id=0, has_side_effects=True, vmem_limit_bytes=56 * 1024 * 1024
        ),
    )(*args)
    return merged.transpose(0, 3, 1, 2, 4)


def solution(mesh):
    in_specs = (
        P(None, None, "lat", "lon", None),
        P(),
        P(),
        P(None, "lat", None, None),
        P(),
        P(),
        P(),
        P(),
        P(),
        P(),
        P(),
    )
    out_specs = P(None, None, "lat", "lon", None)
    return jax.shard_map(body, mesh=mesh, in_specs=in_specs, out_specs=out_specs, check_vma=False)
```
